32 devices in a mesh: seq: 8 (over y, x, core), row: 4 (over z).
Axes of the slice: x: 2, y: 2, z: 4, core: 2. Of those that a mesh axis runs over, the one named last changes fastest.
Arguments:
- inputs: bfloat16 [12, 2048, 1024], P('row', 'seq'), may hold values from -6 to 6
- lengths: int32 [12, 8], P('row'), may hold values from 0 to 2048, as said below
- norm_gain: bfloat16 [1024], P('seq'), may hold values from 0.5 to 1.5
- w_qkv: bfloat16 [1024, 3072], P('seq'), may hold values from -0.1875 to 0.1875
- w_beta: bfloat16 [1024, 8], P('seq'), may hold values from -0.1875 to 0.1875
- beta_bias: bfloat16 [8], replicated, may hold values from -4 to -1
- w_conv: bfloat16 [4, 3072], P(None, 'seq'), may hold values from -2.5 to 2.5
- w_out: bfloat16 [1024, 1024], P('seq'), may hold values from -0.75 to 0.75
- ffn_gain: bfloat16 [1024], P('seq'), may hold values from 0.5 to 1.5
- w_gate: bfloat16 [1024, 2816], P('seq'), may hold values from -0.1875 to 0.1875
- w_up: bfloat16 [1024, 2816], P('seq'), may hold values from -0.1875 to 0.1875
- w_down: bfloat16 [2816, 1024], P('seq'), may hold values from -0.109375 to 0.109375
- cotangent: bfloat16 [12, 2048, 1024], P('row', 'seq'), may hold values from -6 to 6
Outputs:
- output: bfloat16 [12, 2048, 1024], P('row', 'seq')
- grad_inputs: bfloat16 [12, 2048, 1024], P('row', 'seq')
- grad_norm_gain: float32 [1024], P('seq')
- grad_w_qkv: float32 [1024, 3072], P('seq')
- grad_w_beta: float32 [1024, 8], P('seq')
- grad_beta_bias: float32 [8], replicated
- grad_w_conv: float32 [4, 3072], P(None, 'seq')
- grad_w_out: float32 [1024, 1024], P('seq')
- grad_ffn_gain: float32 [1024], P('seq')
- grad_w_gate: float32 [1024, 2816], P('seq')
- grad_w_up: float32 [1024, 2816], P('seq')
- grad_w_down: float32 [2816, 1024], P('seq')
The draws below stay inside these ranges and needn't reach their ends.
Inputs may be any that keep to these rules, and one draw needn't show every extreme that they name: Each row's entries are document lengths laid end to end from the row's first slot, with zeros only after its last nonzero entry; they sum to 2048 at most and the slots after them are padding. In each aligned block of 3 rows one row is a single document of 2048 tokens.
All inputs are finite; a program needn't handle non-finite values.
Results may differ from the reference program's by a relative error of at most 0.019.
Values may be sent and summed in bfloat16 or wider, within the bound.
No kernel may reach another device: no remote copies, remote signals or barrier semaphores. Data moves between devices by JAX's collectives and lax.ppermute only.
A program may use at most 384 MiB of HBM per device.

```python
import jax
import jax.numpy as jnp
from jax import lax

D = 1024
H = 8
DK = 128
FF = 2816
KERN = 4
BLOCK = 64
DOCS = 8
ROWS_DEV = 3
ROW_LEN = 2048
ROWS = 12


def draw_lengths(key, part):
    key = jax.random.fold_in(key, 7)
    keys_all = jax.random.split(key, 4)
    unit_len = max(ROW_LEN // 64, 1)
    group_count = ROWS // ROWS_DEV
    chosen = jax.random.randint(keys_all[0], (group_count,), 0, ROWS_DEV)
    full_row = jnp.arange(ROWS, dtype=jnp.int32) % ROWS_DEV == jnp.repeat(chosen, ROWS_DEV)
    factor = jax.random.randint(keys_all[1], (ROWS, DOCS), 1, 3)
    power = jax.random.randint(keys_all[2], (ROWS, DOCS), 0, 6)
    raw_len = jnp.minimum(unit_len * factor * jnp.left_shift(jnp.ones((ROWS, DOCS), jnp.int32), power), ROW_LEN)
    padding = jax.random.randint(keys_all[3], (ROWS, 1), 1, ROW_LEN // 4 + 1)
    target = ROW_LEN - padding
    doc_ends = jnp.cumsum(raw_len, axis=1, dtype=jnp.int32)
    starting = doc_ends - raw_len
    trimmed = jnp.clip(target - starting, 0, raw_len)
    column = jnp.arange(DOCS, dtype=jnp.int32)[None, :]
    single = jnp.where(column == 0, ROW_LEN, 0)
    return jnp.where(full_row[:, None], single, trimmed).astype(jnp.int32)


def levels(rng, extent, cuts, smallest, largest):
    def one(dim, parts):
        steps = jax.random.uniform(jax.random.fold_in(jax.random.fold_in(rng, 6), dim), (parts,), jnp.float32, smallest / len(cuts), largest / len(cuts))
        return jnp.repeat(jnp.exp(steps), extent[dim] // parts).reshape((-1,) + (1,) * (len(extent) - dim - 1))

    level = one(*cuts[0])
    for cut in cuts[1:]:
        level = level * one(*cut)
    return level


def bell_draw(rng, shape, scale, limit, cuts=(), kind=jnp.bfloat16):
    drawn = scale * jax.random.normal(rng, shape, jnp.float32)
    if cuts:
        drawn = drawn * levels(rng, shape, cuts, -0.22, 0.18)
    return jnp.clip(drawn, -limit, limit).astype(kind)


def setup_inputs(seed: int = 0) -> dict:
    streams_of = jax.random.split(jax.random.key(seed), 14)
    return {
        "inputs": bell_draw(streams_of[0], (ROWS, ROW_LEN, D), 1.0, 6.0, ((0, 4), (1, 8))),
        "lengths": draw_lengths(jax.random.fold_in(streams_of[13], 71), 0),
        "norm_gain": jnp.clip(1.0 + 0.1 * jax.random.normal(streams_of[2], (D,), jnp.float32), 0.5, 1.5).astype(jnp.bfloat16),
        "w_qkv": bell_draw(streams_of[3], (D, 3 * D), D ** -0.5, 0.1875, ((0, 8),)),
        "w_beta": bell_draw(streams_of[4], (D, H), D ** -0.5, 0.1875, ((0, 8),)),
        "beta_bias": jnp.clip(jax.random.uniform(streams_of[5], (H,), jnp.float32, -4.0, -1.0), -4.0, -1.0).astype(jnp.bfloat16),
        "w_conv": bell_draw(streams_of[6], (KERN, 3 * D), 0.5, 2.5, ((1, 8),)),
        "w_out": bell_draw(streams_of[7], (D, D), (D // 16) ** -0.5, 0.75, ((0, 8),)),
        "ffn_gain": jnp.clip(1.0 + 0.1 * jax.random.normal(streams_of[8], (D,), jnp.float32), 0.5, 1.5).astype(jnp.bfloat16),
        "w_gate": bell_draw(streams_of[9], (D, FF), D ** -0.5, 0.1875, ((0, 8),)),
        "w_up": bell_draw(streams_of[10], (D, FF), D ** -0.5, 0.1875, ((0, 8),)),
        "w_down": bell_draw(streams_of[11], (FF, D), FF ** -0.5, 0.109375, ((0, 8),)),
        "cotangent": bell_draw(streams_of[12], (ROWS, ROW_LEN, D), 1.0, 6.0, ((0, 4), (1, 8))),
    }


EPSILON = 1e-06
PRECISE = lax.Precision.HIGHEST

@jax.custom_vjp
def low(v):
    return lax.optimization_barrier(v.astype(jnp.bfloat16)).astype(jnp.float32)

@jax.custom_vjp
def low_back(v):
    return v

def low_keep(v):
    return (low(v), None)

def low_pass(kept, grad):
    return (grad,)

def back_keep(v):
    return (v, None)

def back_low(kept, grad):
    return (low(grad),)
low.defvjp(low_keep, low_pass)
low_back.defvjp(back_keep, back_low)

def rms_scale(values):
    return lax.rsqrt(lax.optimization_barrier(jnp.mean(values * values, axis=-1, keepdims=True)) + EPSILON)

def unit_rows(values):
    return values * lax.rsqrt(lax.optimization_barrier(jnp.sum(values * values, axis=-1, keepdims=True)) + EPSILON)

def block_masks(doc_block, doc_before):
    same_doc = (doc_block[..., :, None] == doc_block[..., None, :]).astype(jnp.float32)
    carried = (doc_block == doc_before[..., None]).astype(jnp.float32)
    last_doc = (doc_block == doc_block[..., -1:]).astype(jnp.float32)
    return (same_doc, carried, last_doc)

def block_weights(key_rows, values, beta_rate, same_doc, carried):
    length = key_rows.shape[-3]
    head_size = key_rows.shape[-1]
    strict = jnp.tril(jnp.ones((length, length), jnp.float32), -1)
    key_gram = jnp.einsum('...thd,...shd->...hts', key_rows, key_rows, precision=PRECISE)
    row_rates = jnp.swapaxes(beta_rate, -1, -2)[..., :, :, None]
    system = key_gram * (same_doc * strict)[..., None, :, :] * row_rates + jnp.eye(length, dtype=jnp.float32)
    right_side = jnp.concatenate([(beta_rate * carried[..., None])[..., None] * key_rows, beta_rate[..., None] * values], axis=-1)
    solved = jax.scipy.linalg.solve_triangular(system, jnp.swapaxes(right_side, -3, -2), lower=True, unit_diagonal=True)
    return (solved[..., :head_size], solved[..., head_size:])

def block_apply(queries, key_rows, weight_keys, weight_values, same_doc, carried, last_doc, memory):
    length = queries.shape[-3]
    inclusive = jnp.tril(jnp.ones((length, length), jnp.float32))
    fresh = weight_values - jnp.einsum('...hcd,...hed->...hce', weight_keys, memory, precision=PRECISE)
    scores = jnp.einsum('...thd,...shd->...hts', queries, key_rows, precision=PRECISE) * (same_doc * inclusive)[..., None, :, :]
    reading = carried[..., :, None, None] * jnp.einsum('...thd,...hed->...the', queries, memory, precision=PRECISE)
    outputs = reading + jnp.einsum('...hts,...hse->...the', scores, fresh, precision=PRECISE)
    last_keys = last_doc[..., :, None, None] * key_rows
    memory = carried[..., -1][..., None, None, None] * memory + jnp.einsum('...hce,...chd->...hed', fresh, last_keys, precision=PRECISE)
    return (outputs, memory)

def delta_rule(queries, key_rows, values, beta_rate, doc_ids):
    length = queries.shape[0]
    block_count = length // BLOCK
    before = jnp.concatenate([jnp.full((1,), -1, jnp.int32), doc_ids[:-1]]).reshape(block_count, BLOCK)[:, 0]
    block_shape = (block_count, BLOCK, H, DK)
    stacked = (queries.reshape(block_shape), key_rows.reshape(block_shape), values.reshape(block_shape), beta_rate.reshape(block_count, BLOCK, H), doc_ids.reshape(block_count, BLOCK), before)

    def advance(memory, block_data):
        block_query, block_key, block_value, block_rate, block_doc, block_before = block_data
        same_doc, carried, last_doc = block_masks(block_doc, block_before)
        weight_keys, weight_values = block_weights(block_key, block_value, block_rate, same_doc, carried)
        outputs, memory = block_apply(block_query, block_key, weight_keys, weight_values, same_doc, carried, last_doc, memory)
        return (memory, outputs)
    initial = jnp.zeros((H, DK, DK), jnp.float32)
    _, outputs = lax.scan(jax.checkpoint(advance), initial, stacked)
    return outputs.reshape(length, H * DK)

def causal_conv(projected, w_conv, doc_ids):
    length = projected.shape[0]
    running = jnp.zeros(projected.shape, jnp.float32)
    for offset in range(KERN):
        moved = jnp.pad(projected, ((offset, 0), (0, 0)))[:length]
        moved_doc = jnp.pad(doc_ids, (offset, 0), constant_values=-1)[:length]
        running = running + w_conv[offset] * moved * (moved_doc == doc_ids).astype(jnp.float32)[:, None]
    return running

def row_forward(valid_mask, doc_ids, inputs, norm_gain, w_qkv, w_beta, beta_bias, w_conv, w_out, ffn_gain, w_gate, w_up, w_down):
    length = inputs.shape[0]
    normed = low(inputs * rms_scale(inputs) * norm_gain)
    projected = low(low_back(jnp.dot(normed, w_qkv, precision=PRECISE)))
    beta_rate = valid_mask[:, None] * jax.nn.sigmoid(jnp.dot(normed, w_beta, precision=PRECISE) + beta_bias)
    convolved = jax.nn.silu(causal_conv(projected, w_conv, doc_ids)).reshape(length, 3, H, DK)
    heads_out = delta_rule(unit_rows(convolved[:, 0]), unit_rows(convolved[:, 1]), convolved[:, 2], beta_rate, doc_ids)
    hidden = inputs + low_back(jnp.dot(low(heads_out), w_out, precision=PRECISE))
    second = low(hidden * rms_scale(hidden) * ffn_gain)
    gated = low_back(jnp.dot(second, w_gate, precision=PRECISE))
    lifted = low_back(jnp.dot(second, w_up, precision=PRECISE))
    activated = low(jax.nn.silu(gated) * lifted)
    return valid_mask[:, None] * (hidden + jnp.dot(activated, w_down, precision=PRECISE))

def doc_layout(lengths, positions):
    doc_ends = jnp.cumsum(lengths, dtype=jnp.int32)
    doc_ids = lax.optimization_barrier(jnp.sum((positions[:, None] >= doc_ends[None, :]).astype(jnp.int32), axis=1, dtype=jnp.int32))
    valid_mask = (positions < doc_ends[-1]).astype(jnp.float32)
    return (doc_ids, valid_mask)

def reference(inputs, lengths, norm_gain, w_qkv, w_beta, beta_bias, w_conv, w_out, ffn_gain, w_gate, w_up, w_down, cotangent):
    weights = tuple((weight.astype(jnp.float32) for weight in (norm_gain, w_qkv, w_beta, beta_bias, w_conv, w_out, ffn_gain, w_gate, w_up, w_down)))
    positions = jnp.arange(ROW_LEN, dtype=jnp.int32)

    def one_row(totals, row_data):
        row_inputs, row_lengths, row_cotangent = row_data
        doc_ids, valid_mask = doc_layout(row_lengths, positions)

        def forward(inputs_wide, *params):
            return row_forward(valid_mask, doc_ids, inputs_wide, *params)
        output, pullback = jax.vjp(forward, row_inputs.astype(jnp.float32), *weights)
        gradients = pullback(row_cotangent.astype(jnp.float32))
        totals = tuple((running + gradient for running, gradient in zip(totals, gradients[1:])))
        return (totals, (output.astype(jnp.bfloat16), gradients[0].astype(jnp.bfloat16)))
    zero_grads = tuple((jnp.zeros(weight.shape, jnp.float32) for weight in weights))
    totals, (outputs, grad_inputs) = lax.scan(one_row, zero_grads, (inputs, lengths, cotangent))
    return (outputs, grad_inputs) + totals
```

```python
import functools

import jax
import jax.numpy as jnp
from jax import lax
from jax.experimental import pallas as pl
from jax.experimental.pallas import tpu as pltpu
from jax.sharding import PartitionSpec as P

EPSILON = 1e-06
LOW = jnp.bfloat16
WIDE = jnp.float32
HEADS_STEP = 4
RIM = 8
VMEM_BYTES = 56 * 1024 * 1024


def nn(left, right):
    return lax.dot_general(
        left.astype(LOW), right.astype(LOW), (((1,), (0,)), ((), ())), preferred_element_type=WIDE
    )


def nt(left, right):
    return lax.dot_general(
        left.astype(LOW), right.astype(LOW), (((1,), (1,)), ((), ())), preferred_element_type=WIDE
    )


def tn(left, right):
    return lax.dot_general(
        left.astype(LOW), right.astype(LOW), (((0,), (0,)), ((), ())), preferred_element_type=WIDE
    )


def split(value):
    high = value.astype(LOW)
    return high, (value - high.astype(WIDE)).astype(LOW)


def nn_fine(left, right):
    left_high, left_low = split(left)
    right_high, right_low = split(right)
    return nn(left_high, right_high) + nn(left_high, right_low) + nn(left_low, right_high)


def rms_scale(values):
    return lax.rsqrt(jnp.mean(values * values, axis=-1, keepdims=True) + EPSILON)


def windows_of(rim, block, taps):
    size = block.shape[0]
    joined = jnp.concatenate([rim, block], axis=0)
    return [block] + [
        pltpu.roll(joined, step, axis=0)[RIM : RIM + size] for step in range(1, taps)
    ]


def convolve(windows, weights, tap_masks):
    total = weights[0:1] * windows[0]
    for step in range(1, len(windows)):
        total = total + weights[step : step + 1] * (windows[step] * tap_masks[step - 1])
    return total


def pair_distance(size):
    row = lax.broadcasted_iota(jnp.int32, (size, size), 0)
    column = lax.broadcasted_iota(jnp.int32, (size, size), 1)
    return row, column


def inverse_unit_lower(strict, row, column):
    size = strict.shape[0]
    apart = row ^ column
    eye = (row == column).astype(WIDE)
    strict_low = strict.astype(LOW)
    result = eye - jnp.where(apart == 1, strict, 0.0)
    level = 1
    while (1 << level) < size:
        corner = jnp.where((apart >> level) == 1, strict, 0.0)
        result_low = result.astype(LOW)
        result = result - nn(result_low, nn(corner, result_low))
        level += 1
    if REFINE:
        result_high, result_rest = split(result)
        rest = (
            eye
            - result
            - nn(strict_low, result_high)
            - nn(strict_low, result_rest)
            - nn(strict - strict_low.astype(WIDE), result_high)
        )
        result = result + nn(result_high, rest)
    return result


REFINE = True


def unit_and_scale(values):
    scale = lax.rsqrt(jnp.sum(values * values, axis=-1, keepdims=True) + EPSILON)
    return values * scale, scale


def head_masks(cols, rows):
    doc_col, doc_row = cols[:, 0:1], rows[0:1, :]
    size = cols.shape[0]
    row, column = pair_distance(size)
    same = doc_col == doc_row
    inclusive = same & (row >= column)
    strict = same & (row > column)
    tap_masks = [cols[:, 1:2], cols[:, 2:3], cols[:, 3:4]]
    return row, column, inclusive, strict, tap_masks, cols[:, 4:5], cols[:, 5:6]


def pick_head(table, head):
    lane = lax.broadcasted_iota(jnp.int32, table.shape, 1)
    return jnp.sum(jnp.where(lane == head, table, 0.0), axis=1, keepdims=True)


def prepare_kernel(
    cols_ref, rows_ref, beta_ref, taps_q, taps_k, taps_v, rim_q, rim_k, rim_v, in_q, in_k, in_v,
    eff_ref, local_ref, maps_ref, solve_ref, weights_ref,
):
    cols, rows = cols_ref[0], rows_ref[0]
    row, column, inclusive, strict, tap_masks, carried, last = head_masks(cols, rows)
    beta_all = beta_ref[0]
    tap_count = taps_q.shape[0]
    for local in range(HEADS_STEP):
        head = pl.program_id(1) * HEADS_STEP + local
        lanes = slice(local * 128, (local + 1) * 128)
        acts = []
        for taps, rim, block in ((taps_q, rim_q, in_q), (taps_k, rim_k, in_k), (taps_v, rim_v, in_v)):
            windows = windows_of(
                rim[0, :, lanes].astype(WIDE), block[0, :, lanes].astype(WIDE), tap_count
            )
            acts.append(jax.nn.silu(convolve(windows, taps[:, lanes].astype(WIDE), tap_masks)))
        query = unit_and_scale(acts[0])[0]
        key = unit_and_scale(acts[1])[0]
        value = acts[2]
        beta = pick_head(beta_all, head)
        gram = nt(jnp.concatenate([key, query], axis=0), key)
        size = key.shape[0]
        system = jnp.where(strict, gram[:size] * beta, 0.0)
        scores = jnp.where(inclusive, gram[size:], 0.0)
        solve = inverse_unit_lower(system, row, column).astype(LOW)
        right = jnp.concatenate([(beta * carried) * key, beta * value], axis=1)
        weights = nn(solve, right).astype(LOW)
        mixed = nn(scores, weights)
        eff_ref[0, local] = (carried * query - mixed[:, :128]).astype(LOW)
        local_ref[0, :, lanes] = mixed[:, 128:]
        maps_ref[0, local] = tn(last * key, weights).astype(LOW)
        solve_ref[0, local] = solve
        weights_ref[0, local] = weights


def prepare_call(cols, rows, beta, taps, rim, projected):
    row_count, size, triple = projected.shape
    head_count = triple // (3 * 128)
    groups = head_count // HEADS_STEP
    wide = HEADS_STEP * 128
    tap_count = taps.shape[0]

    def of_row(block):
        return pl.BlockSpec(block, lambda r, g: (r, 0, 0))

    def part(rows_in, index):
        return pl.BlockSpec((1, rows_in, wide), lambda r, g: (r, 0, index * groups + g))

    def tap_part(index):
        return pl.BlockSpec((tap_count, wide), lambda r, g: (0, index * groups + g))

    def per_head(*block):
        return pl.BlockSpec((1, HEADS_STEP) + block, lambda r, g: (r, g, 0, 0))

    return pl.pallas_call(
        prepare_kernel,
        grid=(row_count, groups),
        in_specs=[of_row((1,) + cols.shape[1:]), of_row((1,) + rows.shape[1:]), of_row((1,) + beta.shape[1:])]
        + [tap_part(i) for i in range(3)]
        + [part(RIM, i) for i in range(3)]
        + [part(size, i) for i in range(3)],
        out_specs=[
            per_head(size, 128),
            pl.BlockSpec((1, size, wide), lambda r, g: (r, 0, g)),
            per_head(128, 256),
            per_head(size, size),
            per_head(size, 256),
        ],
        out_shape=[
            jax.ShapeDtypeStruct((row_count, head_count, size, 128), LOW),
            jax.ShapeDtypeStruct((row_count, size, head_count * 128), WIDE),
            jax.ShapeDtypeStruct((row_count, head_count, 128, 256), LOW),
            jax.ShapeDtypeStruct((row_count, head_count, size, size), LOW),
            jax.ShapeDtypeStruct((row_count, head_count, size, 256), LOW),
        ],
        compiler_params=pltpu.CompilerParams(vmem_limit_bytes=VMEM_BYTES),
        name="prepare",
    )(cols, rows, beta, taps, taps, taps, rim, rim, rim, projected, projected, projected)


def chain_forward_kernel(keep_ref, maps_ref, out_ref):
    count, pairs = maps_ref.shape[0], maps_ref.shape[1]
    states = [jnp.zeros((128, 128), WIDE) for _ in range(pairs)]
    for device in range(count):
        for pair in range(pairs):
            state = states[pair]
            out_ref[device, pair] = state.astype(LOW)
            decay = maps_ref[device, pair, :, :128]
            write = maps_ref[device, pair, :, 128:]
            states[pair] = (
                keep_ref[pair, device] * state - nn(decay, state) + write.astype(WIDE)
            )


def chain_backward_kernel(keep_ref, maps_ref, grads_ref, out_ref):
    count, pairs = maps_ref.shape[0], maps_ref.shape[1]
    states = [jnp.zeros((128, 128), WIDE) for _ in range(pairs)]
    for device in reversed(range(count)):
        for pair in range(pairs):
            state = states[pair]
            out_ref[device, pair] = state.astype(LOW)
            decay = maps_ref[device, pair, :, :128]
            states[pair] = (
                keep_ref[pair, device] * state
                - tn(decay, state)
                + grads_ref[device, pair].astype(WIDE)
            )


def chain_call(kernel, keep, *arrays):
    count, pairs = arrays[0].shape[:2]
    return pl.pallas_call(
        kernel,
        in_specs=[pl.BlockSpec(memory_space=pltpu.SMEM)]
        + [pl.BlockSpec(memory_space=pltpu.VMEM) for _ in arrays],
        out_specs=pl.BlockSpec(memory_space=pltpu.VMEM),
        out_shape=jax.ShapeDtypeStruct((count, pairs, 128, 128), LOW),
        compiler_params=pltpu.CompilerParams(vmem_limit_bytes=VMEM_BYTES),
        name="chain",
    )(keep, *arrays)


def exchange(value, count):
    pairs = value.shape[0]
    share = -(-pairs // count)
    padded = jnp.pad(value, ((0, share * count - pairs),) + ((0, 0),) * (value.ndim - 1))
    cut = padded.reshape((count, share) + value.shape[1:])
    return lax.all_to_all(cut, "seq", split_axis=0, concat_axis=0)


def to_home(value, pairs):
    moved = lax.all_to_all(value, "seq", split_axis=0, concat_axis=0)
    return moved.reshape((-1,) + value.shape[2:])[:pairs]


def read_kernel(eff_ref, local_ref, state_ref, out_ref):
    for local in range(HEADS_STEP):
        lanes = slice(local * 128, (local + 1) * 128)
        out_ref[0, :, lanes] = (
            local_ref[0, :, lanes] + nn(eff_ref[0, local], state_ref[0, local])
        ).astype(LOW)


def read_call(eff, local, state):
    row_count, size, width = local.shape
    groups = width // (128 * HEADS_STEP)
    wide = HEADS_STEP * 128
    return pl.pallas_call(
        read_kernel,
        grid=(row_count, groups),
        in_specs=[
            pl.BlockSpec((1, HEADS_STEP, size, 128), lambda r, g: (r, g, 0, 0)),
            pl.BlockSpec((1, size, wide), lambda r, g: (r, 0, g)),
            pl.BlockSpec((1, HEADS_STEP, 128, 128), lambda r, g: (r, g, 0, 0)),
        ],
        out_specs=pl.BlockSpec((1, size, wide), lambda r, g: (r, 0, g)),
        out_shape=jax.ShapeDtypeStruct((row_count, size, width), LOW),
        compiler_params=pltpu.CompilerParams(vmem_limit_bytes=VMEM_BYTES),
        name="read",
    )(eff, local, state)


def pull_read_kernel(eff_ref, grad_ref, out_ref):
    for local in range(HEADS_STEP):
        lanes = slice(local * 128, (local + 1) * 128)
        out_ref[0, local] = tn(eff_ref[0, local], grad_ref[0, :, lanes]).astype(LOW)


def pull_read_call(eff, grad):
    row_count, size, width = grad.shape
    groups = width // (128 * HEADS_STEP)
    wide = HEADS_STEP * 128
    return pl.pallas_call(
        pull_read_kernel,
        grid=(row_count, groups),
        in_specs=[
            pl.BlockSpec((1, HEADS_STEP, size, 128), lambda r, g: (r, g, 0, 0)),
            pl.BlockSpec((1, size, wide), lambda r, g: (r, 0, g)),
        ],
        out_specs=pl.BlockSpec((1, HEADS_STEP, 128, 128), lambda r, g: (r, g, 0, 0)),
        out_shape=jax.ShapeDtypeStruct((row_count, width // 128, 128, 128), LOW),
        compiler_params=pltpu.CompilerParams(vmem_limit_bytes=VMEM_BYTES),
        name="pull_read",
    )(eff, grad)


def back_kernel(
    cols_ref, rows_ref, beta_ref, taps_q, taps_k, taps_v, rim_q, rim_k, rim_v, in_q, in_k, in_v,
    solve_ref, weights_ref, state_ref, exit_ref, grad_ref,
    out_q, out_k, out_v, edge_q, edge_k, edge_v, tail_q, tail_k, tail_v, tap_q, tap_k, tap_v, rate_ref,
):
    cols, rows = cols_ref[0], rows_ref[0]
    row, column, inclusive, strict, tap_masks, carried, last = head_masks(cols, rows)
    beta_all = beta_ref[0]
    tap_count = taps_q.shape[0]

    @pl.when(pl.program_id(1) == 0)
    def _():
        rate_ref[0] = jnp.zeros(rate_ref.shape[1:], WIDE)

    for local in range(HEADS_STEP):
        head = pl.program_id(1) * HEADS_STEP + local
        lanes = slice(local * 128, (local + 1) * 128)
        moved, acts, slopes = [], [], []
        for taps, rim, block in ((taps_q, rim_q, in_q), (taps_k, rim_k, in_k), (taps_v, rim_v, in_v)):
            windows = windows_of(
                rim[0, :, lanes].astype(WIDE), block[0, :, lanes].astype(WIDE), tap_count
            )
            convolved = convolve(windows, taps[:, lanes].astype(WIDE), tap_masks)
            gate = jax.nn.sigmoid(convolved)
            moved.append(windows)
            acts.append(convolved * gate)
            slopes.append(gate * (1.0 + convolved * (1.0 - gate)))
        query, query_scale = unit_and_scale(acts[0])
        key, key_scale = unit_and_scale(acts[1])
        value = acts[2]
        beta = pick_head(beta_all, head)
        size = key.shape[0]
        state = state_ref[0, local]
        exit_grad = exit_ref[0, local]
        grad_out = grad_ref[0, :, lanes]
        query_low, key_low, grad_low = query.astype(LOW), key.astype(LOW), grad_out.astype(LOW)
        both = jnp.concatenate([key_low, query_low], axis=0)
        gram = nt(both, key_low)
        scores = jnp.where(inclusive, gram[size:], 0.0)
        solve = solve_ref[0, local]
        weights = weights_ref[0, local]
        fresh = weights[:, 128:].astype(WIDE) - nn(weights[:, :128], state)
        fresh_low = fresh.astype(LOW)
        grad_fresh = tn(scores, grad_low) + last * nn(key_low, exit_grad)
        grad_right = tn(solve, grad_fresh)
        right_low = grad_right.astype(LOW)
        sides = jnp.concatenate([right_low, grad_low], axis=0)
        outer = nt(sides, fresh_low)
        grad_system = jnp.where(strict, -outer[:size], 0.0)
        grad_scores = jnp.where(inclusive, outer[size:], 0.0)
        grad_rate = jnp.sum(grad_system * gram[:size], axis=1, keepdims=True)
        grad_gram = beta * grad_system
        grads = jnp.concatenate([grad_gram.astype(LOW), grad_scores.astype(LOW)], axis=0)
        by_key = nn(grads, key_low)
        by_state = nt(sides, state)
        residual = value - carried * nn(key_low, state)
        grad_rate = grad_rate + jnp.sum(grad_right * residual, axis=1, keepdims=True)
        grad_query = carried * by_state[size:] + by_key[size:]
        grad_key = (
            by_key[:size]
            + tn(grads, both)
            + last * nt(fresh_low, exit_grad)
            - (beta * carried) * by_state[:size]
        )
        grad_value = beta * grad_right
        grad_query = query_scale * (
            grad_query - query * jnp.sum(query * grad_query, axis=1, keepdims=True)
        )
        grad_key = key_scale * (grad_key - key * jnp.sum(key * grad_key, axis=1, keepdims=True))
        lane = lax.broadcasted_iota(jnp.int32, rate_ref.shape[1:], 1)
        rate_ref[0] = jnp.where(lane == head, grad_rate, rate_ref[0])
        zeros = jnp.zeros((RIM, 128), WIDE)
        for index, (grad_act, taps, out, edge, tail, tap_out) in enumerate(
            (
                (grad_query, taps_q, out_q, edge_q, tail_q, tap_q),
                (grad_key, taps_k, out_k, edge_k, tail_k, tap_k),
                (grad_value, taps_v, out_v, edge_v, tail_v, tap_v),
            )
        ):
            grad_conv = grad_act * slopes[index]
            weight = taps[:, lanes].astype(WIDE)
            own = weight[0:1] * grad_conv
            edge_sum = zeros
            tap_out[0, 0:1, lanes] = jnp.sum(grad_conv * moved[index][0], axis=0, keepdims=True)
            for step in range(1, tap_count):
                masked = grad_conv * tap_masks[step - 1]
                tap_out[0, step : step + 1, lanes] = jnp.sum(
                    masked * moved[index][step], axis=0, keepdims=True
                )
                joined = jnp.concatenate([zeros, weight[step : step + 1] * masked], axis=0)
                back = pltpu.roll(joined, size + RIM - step, axis=0)
                own = own + back[RIM:]
                edge_sum = edge_sum + back[:RIM]
            out[0, :, lanes] = own.astype(LOW)
            edge[0, :, lanes] = edge_sum
            tail[0, :, lanes] = own[size - RIM :]


def back_call(cols, rows, beta, taps, rim, projected, solve, weights, state, exit_grad, grad):
    row_count, size, triple = projected.shape
    head_count = triple // (3 * 128)
    groups = head_count // HEADS_STEP
    wide = HEADS_STEP * 128
    width = triple // 3
    tap_count = taps.shape[0]

    def of_row(block):
        return pl.BlockSpec(block, lambda r, g: (r, 0, 0))

    def part(rows_in, index):
        return pl.BlockSpec((1, rows_in, wide), lambda r, g: (r, 0, index * groups + g))

    def tap_part(index):
        return pl.BlockSpec((tap_count, wide), lambda r, g: (0, index * groups + g))

    def per_head(*block):
        return pl.BlockSpec((1, HEADS_STEP) + block, lambda r, g: (r, g, 0, 0))

    return pl.pallas_call(
        back_kernel,
        grid=(row_count, groups),
        in_specs=[of_row((1,) + cols.shape[1:]), of_row((1,) + rows.shape[1:]), of_row((1,) + beta.shape[1:])]
        + [tap_part(i) for i in range(3)]
        + [part(RIM, i) for i in range(3)]
        + [part(size, i) for i in range(3)]
        + [per_head(size, size), per_head(size, 256), per_head(128, 128), per_head(128, 128), part(size, 0)],
        out_specs=[part(size, 0)] * 3
        + [part(RIM, 0)] * 6
        + [pl.BlockSpec((1, tap_count, wide), lambda r, g: (r, 0, g))] * 3
        + [of_row((1, size, 128))],
        out_shape=[jax.ShapeDtypeStruct((row_count, size, width), LOW)] * 3
        + [jax.ShapeDtypeStruct((row_count, RIM, width), WIDE)] * 6
        + [jax.ShapeDtypeStruct((row_count, tap_count, width), WIDE)] * 3
        + [jax.ShapeDtypeStruct((row_count, size, 128), WIDE)],
        compiler_params=pltpu.CompilerParams(vmem_limit_bytes=VMEM_BYTES),
        name="mixer_back",
    )(
        cols, rows, beta, taps, taps, taps, rim, rim, rim, projected, projected, projected,
        solve, weights, state, exit_grad, grad,
    )


def shifted(value, axis, steps):
    count = lax.axis_size(axis)
    leading, last = (max(0, -steps), min(count, count - steps))
    return lax.ppermute(value, axis, [(source, source + steps) for source in range(leading, last)])


def on_device(
    inputs,
    lengths,
    norm_gain,
    w_qkv,
    w_beta,
    beta_bias,
    w_conv,
    w_out,
    ffn_gain,
    w_gate,
    w_up,
    w_down,
    cotangent,
):
    row_count, slot_count, width = inputs.shape
    head_count = beta_bias.shape[0]
    tap_count = w_conv.shape[0]
    rim_size = tap_count - 1
    pairs = row_count * head_count
    seq_count = lax.axis_size("seq")
    position = lax.axis_index("seq")
    gather = functools.partial(lax.all_gather, axis_name="seq", tiled=True)
    full_qkv = gather(w_qkv, axis=0)
    small = jnp.concatenate(
        [norm_gain, ffn_gain, w_beta.reshape(-1), w_conv.reshape(-1)], axis=0
    )
    all_small = lax.all_gather(small, "seq", axis=0)
    shard = norm_gain.shape[0]
    full_gain = all_small[:, :shard].reshape(-1)
    full_ffn_gain = all_small[:, shard : 2 * shard].reshape(-1)
    full_beta = all_small[:, 2 * shard : (2 + head_count) * shard].reshape(-1, head_count)
    full_conv = jnp.swapaxes(
        all_small[:, (2 + head_count) * shard :].reshape(seq_count, tap_count, -1), 0, 1
    ).reshape(tap_count, -1)
    full_out = gather(w_out, axis=0)
    full_gate = gather(w_gate, axis=0)
    full_up = gather(w_up, axis=0)
    full_down = gather(w_down, axis=0)

    doc_ends = jnp.cumsum(lengths, axis=1, dtype=jnp.int32)
    spots = position * slot_count - rim_size + jnp.arange(slot_count + rim_size, dtype=jnp.int32)
    ext_docs = jnp.sum(
        (spots[None, :, None] >= doc_ends[:, None, :]).astype(jnp.int32), axis=2, dtype=jnp.int32
    )
    ext_docs = jnp.where(spots[None, :] < 0, -1, ext_docs)
    own_docs = ext_docs[:, rim_size:]
    valid_mask = (spots[None, rim_size:] < doc_ends[:, -1:]).astype(WIDE)
    mask_col = valid_mask[..., None]
    shown = [own_docs.astype(WIDE)]
    for offset in range(1, tap_count):
        before = ext_docs[:, rim_size - offset : rim_size - offset + slot_count]
        shown.append((before == own_docs).astype(WIDE))
    shown.append((own_docs == ext_docs[:, rim_size - 1 : rim_size]).astype(WIDE))
    shown.append((own_docs == own_docs[:, -1:]).astype(WIDE))
    shown += [valid_mask, valid_mask]
    cols = jnp.stack(shown, axis=-1)
    rows = jnp.broadcast_to(own_docs.astype(WIDE)[:, None, :], (row_count, 8, slot_count))
    bounds = jnp.arange(seq_count, dtype=jnp.int32) * slot_count
    doc_first = jnp.sum((bounds[None, :, None] - 1 >= doc_ends[:, None, :]).astype(jnp.int32), axis=2)
    doc_last = jnp.sum(
        (bounds[None, :, None] + slot_count - 1 >= doc_ends[:, None, :]).astype(jnp.int32), axis=2
    )
    keep = (doc_first == doc_last).astype(WIDE)
    share = -(-pairs // seq_count)
    keep_pairs = jnp.pad(
        jnp.repeat(keep, head_count, axis=0), ((0, share * seq_count - pairs), (0, 0))
    )
    keep_own = lax.dynamic_slice_in_dim(keep_pairs, position * share, share, axis=0)

    wide_inputs = inputs.astype(WIDE)
    first_scale = rms_scale(wide_inputs)
    normed = (wide_inputs * first_scale * full_gain).astype(LOW)
    projected = jnp.dot(normed, full_qkv, preferred_element_type=WIDE).astype(LOW)
    logits = jnp.dot(normed, full_beta, preferred_element_type=WIDE) + beta_bias.astype(WIDE)
    beta_open = jax.nn.sigmoid(logits)
    beta_rate = mask_col * beta_open
    rim_rows = shifted(projected[:, slot_count - rim_size :], "seq", 1)
    rim = jnp.pad(rim_rows, ((0, 0), (RIM - rim_size, 0), (0, 0)))

    eff, local_out, maps, solve, weights = prepare_call(
        cols, rows, beta_rate, full_conv, rim, projected
    )
    maps_here = exchange(maps.reshape((pairs,) + maps.shape[2:]), seq_count)
    states_here = chain_call(chain_forward_kernel, keep_own, maps_here)
    state = to_home(states_here, pairs).reshape((row_count, head_count, 128, 128))
    heads_low = read_call(eff, local_out, state)

    hidden = wide_inputs + jnp.dot(heads_low, full_out, preferred_element_type=WIDE)
    second_scale = rms_scale(hidden)
    second = (hidden * second_scale * full_ffn_gain).astype(LOW)
    gated = jnp.dot(second, full_gate, preferred_element_type=WIDE)
    lifted = jnp.dot(second, full_up, preferred_element_type=WIDE)
    activated = (jax.nn.silu(gated) * lifted).astype(LOW)
    output = (
        mask_col * (hidden + jnp.dot(activated, full_down, preferred_element_type=WIDE))
    ).astype(LOW)
    upstream = cotangent.astype(WIDE) * mask_col
    upstream_low = upstream.astype(LOW)
    grad_act = jnp.einsum("rsd,fd->rsf", upstream_low, full_down, preferred_element_type=WIDE)
    sigmoid_gate = jax.nn.sigmoid(gated)
    grad_gated = (grad_act * lifted * sigmoid_gate * (1.0 + gated * (1.0 - sigmoid_gate))).astype(LOW)
    grad_lifted = (grad_act * gated * sigmoid_gate).astype(LOW)
    grad_second = jnp.einsum(
        "rsf,df->rsd", grad_gated, full_gate, preferred_element_type=WIDE
    ) + jnp.einsum("rsf,df->rsd", grad_lifted, full_up, preferred_element_type=WIDE)
    grad_ffn_gain = jnp.sum(grad_second * hidden * second_scale, axis=(0, 1))
    scaled_second = full_ffn_gain.astype(WIDE) * grad_second
    grad_hidden = (
        upstream
        + second_scale * scaled_second
        - hidden * second_scale**3 * jnp.mean(scaled_second * hidden, axis=-1, keepdims=True)
    )
    grad_mix_low = grad_hidden.astype(LOW)
    grad_heads = jnp.einsum("rse,de->rsd", grad_mix_low, full_out, preferred_element_type=WIDE)
    grad_heads = grad_heads.astype(LOW)

    local_grad = pull_read_call(eff, grad_heads)
    grads_here = exchange(local_grad.reshape((pairs, 128, 128)), seq_count)
    exits_here = chain_call(chain_backward_kernel, keep_own, maps_here, grads_here)
    exit_grad = to_home(exits_here, pairs).reshape((row_count, head_count, 128, 128))

    scatter = functools.partial(lax.psum_scatter, axis_name="seq", scatter_dimension=0, tiled=True)
    grad_down = jnp.einsum("rsf,rsd->fd", activated, upstream_low, preferred_element_type=WIDE)
    grad_gate_w = jnp.einsum("rsd,rsf->df", second, grad_gated, preferred_element_type=WIDE)
    grad_up_w = jnp.einsum("rsd,rsf->df", second, grad_lifted, preferred_element_type=WIDE)
    grad_out_w = jnp.einsum("rsd,rse->de", heads_low, grad_mix_low, preferred_element_type=WIDE)
    shard_down = scatter(grad_down.astype(LOW))
    shard_gate = scatter(grad_gate_w.astype(LOW))
    shard_up = scatter(grad_up_w.astype(LOW))
    shard_out = scatter(grad_out_w.astype(LOW))

    pulled = back_call(
        cols, rows, beta_rate, full_conv, rim, projected, solve, weights, state, exit_grad, grad_heads
    )
    grad_parts, edges, tails, tap_sums, rate = (
        pulled[0:3], pulled[3:6], pulled[6:9], pulled[9:12], pulled[12]
    )
    back_rim = shifted(
        jnp.concatenate([edge[:, RIM - rim_size :] for edge in edges], axis=-1).astype(LOW), "seq", -1
    ).astype(WIDE)
    fixed = []
    for index in range(3):
        tail = tails[index][:, RIM - rim_size :] + back_rim[:, :, index * width : (index + 1) * width]
        fixed.append(
            lax.dynamic_update_slice(
                grad_parts[index], tail.astype(LOW), (0, slot_count - rim_size, 0)
            )
        )
    grad_conv_w = jnp.concatenate([jnp.sum(tap, axis=0) for tap in tap_sums], axis=-1)
    grad_logits = rate[:, :, :head_count] * beta_rate * (1.0 - beta_open)

    grad_qkv_w = [
        jnp.einsum("rsd,rse->de", normed, part, preferred_element_type=WIDE) for part in fixed
    ]
    shard_qkv = jnp.concatenate([scatter(part.astype(LOW)) for part in grad_qkv_w], axis=-1)
    grad_beta_w = jnp.einsum(
        "rsd,rsh->dh", normed.astype(WIDE), grad_logits, precision=lax.Precision.HIGHEST
    )
    bias_local = jnp.sum(grad_logits, axis=(0, 1))
    grad_normed = jnp.einsum(
        "rsh,dh->rsd", grad_logits, full_beta.astype(WIDE), precision=lax.Precision.HIGHEST
    )
    for index in range(3):
        grad_normed = grad_normed + jnp.einsum(
            "rse,de->rsd",
            fixed[index],
            full_qkv[:, index * width : (index + 1) * width],
            preferred_element_type=WIDE,
        )
    grad_norm_gain = jnp.sum(grad_normed * wide_inputs * first_scale, axis=(0, 1))
    scaled_first = full_gain.astype(WIDE) * grad_normed
    grad_inputs = (
        grad_hidden
        + first_scale * scaled_first
        - wide_inputs
        * first_scale**3
        * jnp.mean(scaled_first * wide_inputs, axis=-1, keepdims=True)
    )
    minor = jnp.concatenate(
        [
            grad_norm_gain.reshape(seq_count, -1),
            grad_ffn_gain.reshape(seq_count, -1),
            grad_beta_w.reshape(seq_count, -1),
            jnp.swapaxes(grad_conv_w.reshape(tap_count, seq_count, -1), 0, 1).reshape(seq_count, -1),
            jnp.broadcast_to(bias_local[None], (seq_count, head_count)),
        ],
        axis=1,
    )
    minor_total = lax.psum(lax.psum_scatter(minor, "seq", scatter_dimension=0, tiled=True), "row")[0]
    total = [
        lax.psum(shard, "row").astype(WIDE)
        for shard in (shard_qkv, shard_out, shard_gate, shard_up, shard_down)
    ]
    cuts = [shard, 2 * shard, (2 + head_count) * shard, minor_total.shape[0] - head_count]
    return (
        output,
        grad_inputs.astype(LOW),
        minor_total[: cuts[0]],
        total[0],
        minor_total[cuts[1] : cuts[2]].reshape(shard, head_count),
        minor_total[cuts[3] :],
        minor_total[cuts[2] : cuts[3]].reshape(tap_count, -1),
        total[1],
        minor_total[cuts[0] : cuts[1]],
        total[2],
        total[3],
        total[4],
    )


def solution(mesh):
    placed = (
        P("row", "seq", None),
        P("row", None),
        P("seq"),
        P("seq", None),
        P("seq", None),
        P(),
        P(None, "seq"),
        P("seq", None),
        P("seq"),
        P("seq", None),
        P("seq", None),
        P("seq", None),
        P("row", "seq", None),
    )
    return jax.shard_map(
        on_device,
        mesh=mesh,
        in_specs=placed,
        out_specs=(
            P("row", "seq", None),
            P("row", "seq", None),
            P("seq"),
            P("seq", None),
            P("seq", None),
            P(),
            P(None, "seq"),
            P("seq", None),
            P("seq"),
            P("seq", None),
            P("seq", None),
            P("seq", None),
        ),
        check_vma=False,
    )
```

```python
import functools

import jax
import jax.numpy as jnp
from jax import lax
from jax.experimental import pallas as pl
from jax.experimental.pallas import tpu as pltpu
from jax.sharding import PartitionSpec as P

EPSILON = 1e-06
LOW = jnp.bfloat16
WIDE = jnp.float32
HEADS_STEP = 8
RIM = 8
VMEM_BYTES = 56 * 1024 * 1024


def nn(left, right):
    return lax.dot_general(
        left.astype(LOW), right.astype(LOW), (((1,), (0,)), ((), ())), preferred_element_type=WIDE
    )


def nt(left, right):
    return lax.dot_general(
        left.astype(LOW), right.astype(LOW), (((1,), (1,)), ((), ())), preferred_element_type=WIDE
    )


def tn(left, right):
    return lax.dot_general(
        left.astype(LOW), right.astype(LOW), (((0,), (0,)), ((), ())), preferred_element_type=WIDE
    )


def split(value):
    high = value.astype(LOW)
    return high, (value - high.astype(WIDE)).astype(LOW)


def nn_fine(left, right):
    left_high, left_low = split(left)
    right_high, right_low = split(right)
    return nn(left_high, right_high) + nn(left_high, right_low) + nn(left_low, right_high)


def rms_scale(values):
    return lax.rsqrt(jnp.mean(values * values, axis=-1, keepdims=True) + EPSILON)


def windows_of(rim, block, taps, room):
    size = block.shape[0]
    room[pl.ds(0, RIM), :] = rim
    room[pl.ds(RIM, size), :] = block
    return [block] + [room[pl.ds(RIM - step, size), :] for step in range(1, taps)]


def convolve(windows, weights, tap_masks):
    total = weights[0:1] * windows[0]
    for step in range(1, len(windows)):
        total = total + weights[step : step + 1] * (windows[step] * tap_masks[step - 1])
    return total


def pair_distance(size):
    row = lax.broadcasted_iota(jnp.int32, (size, size), 0)
    column = lax.broadcasted_iota(jnp.int32, (size, size), 1)
    return row, column


def inverse_unit_lower(stricts, corners):
    size = stricts[0].shape[0]
    row, column = pair_distance(size)
    eye = (row == column).astype(WIDE)
    results = [eye - strict * corners[0] for strict in stricts]
    level = 1
    while (1 << level) < size:
        lows = [result.astype(LOW) for result in results]
        halves = [
            nn((strict * corners[level]).astype(LOW), low).astype(LOW)
            for strict, low in zip(stricts, lows)
        ]
        results = [
            result - nn(low, half) for result, low, half in zip(results, lows, halves)
        ]
        level += 1
    if REFINE:
        rests = []
        for strict, result in zip(stricts, results):
            high, low = split(result)
            strict_high, strict_low = split(strict)
            rests.append(
                eye - result - nn(strict_high, high) - nn(strict_high, low) - nn(strict_low, high)
            )
        results = [result + nn(result, rest) for result, rest in zip(results, rests)]
    return results


REFINE = True


def unit_and_scale(values):
    scale = lax.rsqrt(jnp.sum(values * values, axis=-1, keepdims=True) + EPSILON)
    return values * scale, scale


def head_masks(cols, rows):
    doc_col, doc_row = cols[:, 0:1], rows[0:1, :]
    size = cols.shape[0]
    row, column = pair_distance(size)
    same = doc_col == doc_row
    inclusive = same & (row >= column)
    strict = same & (row > column)
    tap_masks = [cols[:, 1:2], cols[:, 2:3], cols[:, 3:4]]
    return row, column, inclusive, strict, tap_masks, cols[:, 4:5], cols[:, 5:6]


def pick_head(table, head):
    lane = lax.broadcasted_iota(jnp.int32, table.shape, 1)
    return jnp.sum(jnp.where(lane == head, table, 0.0), axis=1, keepdims=True)


def prepare_kernel(
    cols_ref, rows_ref, beta_ref, taps_q, taps_k, taps_v, rim_q, rim_k, rim_v, in_q, in_k, in_v,
    eff_ref, local_ref, maps_ref, solve_ref, weights_ref, room_ref,
):
    cols, rows = cols_ref[0], rows_ref[0]
    row, column, inclusive, strict, tap_masks, carried, last = head_masks(cols, rows)
    beta_all = beta_ref[0]
    tap_count = taps_q.shape[0]
    size = cols.shape[0]
    half = size // 2
    apart = (row ^ column)[:half, :half]
    corners = []
    level = 0
    while (1 << level) < half:
        corners.append(((apart >> level) == 1).astype(WIDE))
        level += 1
    heads = range(HEADS_STEP)
    lanes = [slice(local * 128, (local + 1) * 128) for local in heads]
    queries, keys, values, betas = [], [], [], []
    for local in heads:
        acts = []
        for index, (taps, rim, block) in enumerate(
            ((taps_q, rim_q, in_q), (taps_k, rim_k, in_k), (taps_v, rim_v, in_v))
        ):
            windows = windows_of(
                rim[0, :, lanes[local]].astype(WIDE),
                block[0, :, lanes[local]].astype(WIDE),
                tap_count,
                room_ref.at[3 * local + index],
            )
            acts.append(jax.nn.silu(convolve(windows, taps[:, lanes[local]].astype(WIDE), tap_masks)))
        queries.append(unit_and_scale(acts[0])[0])
        keys.append(unit_and_scale(acts[1])[0])
        values.append(acts[2])
        betas.append(pick_head(beta_all, pl.program_id(1) * HEADS_STEP + local))
    grams = [
        nt(jnp.concatenate([key.astype(LOW), query.astype(LOW)], axis=0), key)
        for key, query in zip(keys, queries)
    ]
    systems = [jnp.where(strict, gram[:size] * beta, 0.0) for gram, beta in zip(grams, betas)]
    scores = [jnp.where(inclusive, gram[size:], 0.0).astype(LOW) for gram in grams]
    blocks = inverse_unit_lower(
        [system[:half, :half] for system in systems] + [system[half:, half:] for system in systems],
        corners,
    )
    upper = [block.astype(LOW) for block in blocks[:HEADS_STEP]]
    lower = [block.astype(LOW) for block in blocks[HEADS_STEP:]]
    crossing = [nn(system[half:, :half], block) for system, block in zip(systems, upper)]
    crossing = [-nn(block, cross) for block, cross in zip(lower, crossing)]
    solves = [
        jnp.concatenate(
            [
                jnp.concatenate([first, jnp.zeros((half, half), LOW)], axis=1),
                jnp.concatenate([cross.astype(LOW), second], axis=1),
            ],
            axis=0,
        )
        for first, second, cross in zip(upper, lower, crossing)
    ]
    rights = [
        jnp.concatenate([(beta * carried) * key, beta * value], axis=1)
        for beta, key, value in zip(betas, keys, values)
    ]
    weights = [nn(solve, right).astype(LOW) for solve, right in zip(solves, rights)]
    mixed = [nn(score, weight) for score, weight in zip(scores, weights)]
    maps = [tn(last * key, weight) for key, weight in zip(keys, weights)]
    for local in heads:
        eff_ref[0, local] = (carried * queries[local] - mixed[local][:, :128]).astype(LOW)
        local_ref[0, :, lanes[local]] = mixed[local][:, 128:]
        maps_ref[0, local] = maps[local].astype(LOW)
        solve_ref[0, local] = solves[local]
        weights_ref[0, local] = weights[local]


def prepare_call(cols, rows, beta, taps, rim, projected):
    row_count, size, triple = projected.shape
    head_count = triple // (3 * 128)
    groups = head_count // HEADS_STEP
    wide = HEADS_STEP * 128
    tap_count = taps.shape[0]

    def of_row(block):
        return pl.BlockSpec(block, lambda r, g: (r, 0, 0))

    def part(rows_in, index):
        return pl.BlockSpec((1, rows_in, wide), lambda r, g: (r, 0, index * groups + g))

    def tap_part(index):
        return pl.BlockSpec((tap_count, wide), lambda r, g: (0, index * groups + g))

    def per_head(*block):
        return pl.BlockSpec((1, HEADS_STEP) + block, lambda r, g: (r, g, 0, 0))

    return pl.pallas_call(
        prepare_kernel,
        grid=(row_count, groups),
        in_specs=[of_row((1,) + cols.shape[1:]), of_row((1,) + rows.shape[1:]), of_row((1,) + beta.shape[1:])]
        + [tap_part(i) for i in range(3)]
        + [part(RIM, i) for i in range(3)]
        + [part(size, i) for i in range(3)],
        out_specs=[
            per_head(size, 128),
            pl.BlockSpec((1, size, wide), lambda r, g: (r, 0, g)),
            per_head(128, 256),
            per_head(size, size),
            per_head(size, 256),
        ],
        out_shape=[
            jax.ShapeDtypeStruct((row_count, head_count, size, 128), LOW),
            jax.ShapeDtypeStruct((row_count, size, head_count * 128), WIDE),
            jax.ShapeDtypeStruct((row_count, head_count, 128, 256), LOW),
            jax.ShapeDtypeStruct((row_count, head_count, size, size), LOW),
            jax.ShapeDtypeStruct((row_count, head_count, size, 256), LOW),
        ],
        scratch_shapes=[pltpu.VMEM((3 * HEADS_STEP, RIM + size, 128), WIDE)],
        compiler_params=pltpu.CompilerParams(vmem_limit_bytes=VMEM_BYTES),
        cost_estimate=timed(22),
        name="prepare",
    )(cols, rows, beta, taps, taps, taps, rim, rim, rim, projected, projected, projected)


def chain_forward_kernel(keep_ref, maps_ref, out_ref):
    count, pairs = maps_ref.shape[0], maps_ref.shape[1]
    states = [jnp.zeros((128, 128), WIDE) for _ in range(pairs)]
    for device in range(count):
        for pair in range(pairs):
            state = states[pair]
            out_ref[device, pair] = state.astype(LOW)
            decay = maps_ref[device, pair, :, :128]
            write = maps_ref[device, pair, :, 128:]
            states[pair] = (
                keep_ref[pair, device] * state - nn(decay, state) + write.astype(WIDE)
            )


def chain_backward_kernel(keep_ref, maps_ref, grads_ref, out_ref):
    count, pairs = maps_ref.shape[0], maps_ref.shape[1]
    states = [jnp.zeros((128, 128), WIDE) for _ in range(pairs)]
    for device in reversed(range(count)):
        for pair in range(pairs):
            state = states[pair]
            out_ref[device, pair] = state.astype(LOW)
            decay = maps_ref[device, pair, :, :128]
            states[pair] = (
                keep_ref[pair, device] * state
                - tn(decay, state)
                + grads_ref[device, pair].astype(WIDE)
            )


def chain_call(kernel, keep, *arrays):
    count, pairs = arrays[0].shape[:2]
    return pl.pallas_call(
        kernel,
        in_specs=[pl.BlockSpec(memory_space=pltpu.SMEM)]
        + [pl.BlockSpec(memory_space=pltpu.VMEM) for _ in arrays],
        out_specs=pl.BlockSpec(memory_space=pltpu.VMEM),
        out_shape=jax.ShapeDtypeStruct((count, pairs, 128, 128), LOW),
        compiler_params=pltpu.CompilerParams(vmem_limit_bytes=VMEM_BYTES),
        cost_estimate=timed(3),
        name="chain",
    )(keep, *arrays)


def exchange(value, count):
    pairs = value.shape[0]
    share = -(-pairs // count)
    padded = jnp.pad(value, ((0, share * count - pairs),) + ((0, 0),) * (value.ndim - 1))
    cut = padded.reshape((count, share) + value.shape[1:])
    return lax.all_to_all(cut, "seq", split_axis=0, concat_axis=0)


def to_home(value, pairs):
    moved = lax.all_to_all(value, "seq", split_axis=0, concat_axis=0)
    return moved.reshape((-1,) + value.shape[2:])[:pairs]


def feed_kernel(
    gate_moves, up_moves, position_ref, eff_ref, local_ref, state_ref, inputs_ref, cot_ref, valid_ref, gain_ref, w_out_ref,
    down_ref, *refs,
):
    count = len(gate_moves)
    (
    heads_ref, second_ref, act_ref, pair_ref, output_ref, upstream_ref,
    hidden_grad_ref, mix_ref, heads_grad_ref, local_grad_ref, gain_grad_ref,
    hidden_ref, out_sum, second_sum, gate_ref, up_ref,
    ) = refs[count + len(up_moves) :]
    put([gate_ref], refs[:count], gate_moves, position_ref[0])
    put([up_ref], refs[count : count + len(up_moves)], up_moves, position_ref[0])
    step, last_step = pl.program_id(0), pl.num_programs(0) - 1
    row_count, head_count, size = eff_ref.shape[:3]

    @pl.when(step == 0)
    def _():
        for r in range(row_count):
            tokens = slice(r * size, (r + 1) * size)
            for h in range(head_count):
                lanes = slice(h * 128, (h + 1) * 128)
                heads_ref[tokens, lanes] = (
                    local_ref[r, :, lanes] + nn(eff_ref[r, h], state_ref[r, h])
                ).astype(LOW)
        hidden = inputs_ref[...].astype(WIDE) + nn(heads_ref[...], w_out_ref[...])
        hidden_ref[...] = hidden
        second_ref[...] = (hidden * rms_scale(hidden) * gain_ref[...]).astype(LOW)
        upstream_ref[...] = (cot_ref[...].astype(WIDE) * valid_ref[:, 0:1]).astype(LOW)
        out_sum[...] = hidden
        second_sum[...] = jnp.zeros(second_sum.shape, WIDE)

    second = second_ref[...]
    gated = nn(second, gate_ref[...])
    lifted = nn(second, up_ref[...])
    grad_act = nt(upstream_ref[...], down_ref[...])
    gate = jax.nn.sigmoid(gated)
    opened = gated * gate
    act = (opened * lifted).astype(LOW)
    act_ref[...] = act
    grad_gated = (grad_act * lifted * gate * (1.0 + gated * (1.0 - gate))).astype(LOW)
    grad_lifted = (grad_act * opened).astype(LOW)
    pair_ref[0] = grad_gated
    pair_ref[1] = grad_lifted
    out_sum[...] += nn(act, down_ref[...])
    second_sum[...] += nt(grad_gated, gate_ref[...]) + nt(grad_lifted, up_ref[...])

    @pl.when(step == last_step)
    def _():
        output_ref[...] = (valid_ref[:, 0:1] * out_sum[...]).astype(LOW)
        hidden = hidden_ref[...]
        scale = rms_scale(hidden)
        grad_second = second_sum[...]
        gain_grad_ref[...] = jnp.sum(grad_second * hidden * scale, axis=0, keepdims=True)
        scaled = gain_ref[...] * grad_second
        grad_hidden = (
            upstream_ref[...].astype(WIDE)
            + scale * scaled
            - hidden * (scale * scale * scale * jnp.mean(scaled * hidden, axis=-1, keepdims=True))
        )
        hidden_grad_ref[...] = grad_hidden
        mix_ref[...] = grad_hidden.astype(LOW)
        heads_grad_ref[...] = nt(mix_ref[...], w_out_ref[...]).astype(LOW)
        for r in range(row_count):
            tokens = slice(r * size, (r + 1) * size)
            for h in range(head_count):
                lanes = slice(h * 128, (h + 1) * 128)
                local_grad_ref[r, h] = tn(eff_ref[r, h], heads_grad_ref[tokens, lanes]).astype(LOW)


def feed_call(eff, local, state, inputs, cot, valid, gain, w_out, gate, up, w_down):
    row_count, head_count, size = eff.shape[:3]
    tokens, width = inputs.shape
    pieces, position = gate[0] + up[0], gate[3]
    units = pieces[0].shape[1]
    tile = FEED_TILE

    def whole(shape):
        return pl.BlockSpec(shape, lambda j: (0,) * len(shape), pipeline_mode=pl.Buffered(1))

    token_low = jax.ShapeDtypeStruct((tokens, width), LOW)
    token_spec = whole((tokens, width))
    return pl.pallas_call(
        functools.partial(feed_kernel, gate[1], up[1]),
        grid=(units // tile,),
        in_specs=[
            pl.BlockSpec(memory_space=pltpu.SMEM), whole(eff.shape), whole(local.shape), whole(state.shape), token_spec, token_spec,
            whole(valid.shape), whole(gain.shape), whole(w_out.shape),
            pl.BlockSpec((tile, width), lambda j: (j, 0)),
        ]
        + [pl.BlockSpec((piece.shape[0], tile), lambda j: (0, j)) for piece in pieces],
        out_specs=[
            token_spec, token_spec,
            pl.BlockSpec((tokens, tile), lambda j: (0, j)),
            pl.BlockSpec((2, tokens, tile), lambda j: (0, 0, j)),
            token_spec, token_spec, token_spec, token_spec, token_spec,
            whole(state.shape), whole((1, width)),
        ],
        out_shape=[
            token_low, token_low,
            jax.ShapeDtypeStruct((tokens, units), LOW),
            jax.ShapeDtypeStruct((2, tokens, units), LOW),
            token_low, token_low,
            jax.ShapeDtypeStruct((tokens, width), WIDE),
            token_low, token_low,
            jax.ShapeDtypeStruct(state.shape, LOW),
            jax.ShapeDtypeStruct((1, width), WIDE),
        ],
        scratch_shapes=[pltpu.VMEM((tokens, width), WIDE)] * 3 + [pltpu.VMEM((width, tile), LOW)] * 2,
        compiler_params=pltpu.CompilerParams(vmem_limit_bytes=VMEM_BYTES),
        cost_estimate=timed(38),
        name="feed",
    )(position, eff, local, state, inputs, cot, valid, gain, w_out, w_down, *pieces)


FEED_TILE = 256


def project_back_kernel(
    first_ref, second_ref, weight_ref, logit_ref, extra_ref, inputs_ref, gain_ref, hidden_grad_ref,
    out_ref, gain_grad_ref, total,
):
    step = pl.program_id(0)
    half = first_ref.shape[2]

    @pl.when(step == 0)
    def _():
        high, low = split(logit_ref[...])
        total[...] = nt(high, extra_ref[...]) + nt(low, extra_ref[...])

    total[...] += nt(first_ref[0], weight_ref[:, :half]) + nt(second_ref[0], weight_ref[:, half:])

    @pl.when(step == pl.num_programs(0) - 1)
    def _():
        inputs = inputs_ref[...].astype(WIDE)
        scale = rms_scale(inputs)
        grad = total[...]
        gain_grad_ref[...] = jnp.sum(grad * inputs * scale, axis=0, keepdims=True)
        scaled = gain_ref[...] * grad
        out_ref[...] = (
            hidden_grad_ref[...]
            + scale * scaled
            - inputs * (scale * scale * scale * jnp.mean(scaled * inputs, axis=-1, keepdims=True))
        ).astype(LOW)


def project_back_call(first, second, joint, grad_logits, extra, inputs, gain, hidden_grad):
    parts, tokens, half = first.shape
    width = 2 * half

    def whole(shape):
        return pl.BlockSpec(shape, lambda j: (0,) * len(shape))

    return pl.pallas_call(
        project_back_kernel,
        grid=(parts,),
        in_specs=[
            pl.BlockSpec((1, tokens, half), lambda j: (j, 0, 0)),
            pl.BlockSpec((1, tokens, half), lambda j: (j, 0, 0)),
            pl.BlockSpec((width, width), lambda j: (0, j)),
            whole((tokens, 128)), whole((width, 128)),
            whole((tokens, width)), whole((1, width)), whole((tokens, width)),
        ],
        out_specs=[whole((tokens, width)), whole((1, width))],
        out_shape=[
            jax.ShapeDtypeStruct((tokens, width), LOW),
            jax.ShapeDtypeStruct((1, width), WIDE),
        ],
        scratch_shapes=[pltpu.VMEM((tokens, width), WIDE)],
        compiler_params=pltpu.CompilerParams(vmem_limit_bytes=VMEM_BYTES),
        cost_estimate=timed(10),
        name="project_back",
    )(first, second, joint, grad_logits, extra, inputs, gain, hidden_grad)


def back_kernel(
    first_head, cols_ref, rows_ref, beta_ref, taps_q, taps_k, taps_v, rim_q, rim_k, rim_v, in_q, in_k, in_v,
    solve_ref, weights_ref, state_ref, exit_ref, grad_ref,
    out_ref, edge_ref, tail_ref, tap_ref, rate_ref, room_ref, back_ref,
):
    cols, rows = cols_ref[0], rows_ref[0]
    row, column, inclusive, strict, tap_masks, carried, last = head_masks(cols, rows)
    beta_all = beta_ref[0]
    tap_count = taps_q.shape[0]
    size = cols.shape[0]
    heads = range(state_ref.shape[1])
    lanes = [slice(local * 128, (local + 1) * 128) for local in heads]
    parts = ((taps_q, rim_q, in_q), (taps_k, rim_k, in_k), (taps_v, rim_v, in_v))

    queries, keys, values, betas, kept = [], [], [], [], []
    for local in heads:
        acts = []
        for index, (taps, rim, block) in enumerate(parts):
            windows = windows_of(
                rim[0, :, lanes[local]].astype(WIDE),
                block[0, :, lanes[local]].astype(WIDE),
                tap_count,
                room_ref.at[3 * local + index],
            )
            convolved = convolve(windows, taps[:, lanes[local]].astype(WIDE), tap_masks)
            gate = jax.nn.sigmoid(convolved)
            acts.append(convolved * gate)
            kept.append(gate * (1.0 + convolved * (1.0 - gate)))
        queries.append(unit_and_scale(acts[0]))
        keys.append(unit_and_scale(acts[1]))
        values.append(acts[2])
        betas.append(pick_head(beta_all, first_head + local))
    eye = (row == column).astype(LOW)
    strict_low = jnp.where(strict, 1.0, 0.0).astype(LOW)
    inclusive_low = jnp.where(inclusive, 1.0, 0.0).astype(LOW)
    later_low = jnp.where(rows[0:1, :] == cols[:, 0:1], jnp.where(row <= column, 1.0, 0.0), 0.0).astype(LOW)
    later_strict_low = later_low - eye
    key_lows = [key.astype(LOW) for key, _ in keys]
    query_lows = [query.astype(LOW) for query, _ in queries]
    boths = [jnp.concatenate([key, query], axis=0) for key, query in zip(key_lows, query_lows)]
    grad_lows = [grad_ref[0, :, lanes[local]] for local in heads]
    scores_turned = [
        nt(key, query).astype(LOW) * later_low for key, query in zip(key_lows, query_lows)
    ]
    by_states = [nn(key_lows[i], state_ref[0, i]) for i in heads]
    freshes = [
        (weights_ref[0, i, :, 128:].astype(WIDE) - nn(weights_ref[0, i, :, :128], state_ref[0, i])).astype(LOW)
        for i in heads
    ]
    from_exit = [nn(key_lows[i], exit_ref[0, i]) for i in heads]
    solves_turned = [nt(eye, solve_ref[0, i]).astype(LOW) for i in heads]
    grad_fresh = [nn(scores_turned[i], grad_lows[i]) + last * from_exit[i] for i in heads]
    grad_right = [nn(solves_turned[i], grad_fresh[i]) for i in heads]
    sides = [
        jnp.concatenate([right.astype(LOW), grad], axis=0) for right, grad in zip(grad_right, grad_lows)
    ]
    outers = [nt(side, fresh).astype(LOW) for side, fresh in zip(sides, freshes)]
    outers_turned = [nt(fresh, side).astype(LOW) for side, fresh in zip(sides, freshes)]
    side_states = [nt(sides[i], state_ref[0, i]) for i in heads]
    grads = [
        jnp.concatenate([outer[:size] * strict_low, outer[size:] * inclusive_low], axis=0)
        for outer in outers
    ]
    grads_turned = [
        jnp.concatenate([outer[:, :size] * later_strict_low, outer[:, size:] * later_low], axis=1)
        for outer in outers_turned
    ]
    by_keys = [nn(grad, key) for grad, key in zip(grads, key_lows)]
    by_both = [
        nn(grads_turned[i], jnp.concatenate([(-betas[i] * keys[i][0]).astype(LOW), query_lows[i]], axis=0))
        for i in heads
    ]
    to_exit = [nt(freshes[i], exit_ref[0, i]) for i in heads]
    rates = [
        jnp.sum(
            grad_right[i] * (values[i] - carried * by_states[i]) - by_keys[i][:size] * keys[i][0],
            axis=1,
            keepdims=True,
        )
        for i in heads
    ]
    lane = lax.broadcasted_iota(jnp.int32, rate_ref.shape[1:], 1)
    rate_sum = jnp.zeros(rate_ref.shape[1:], WIDE)
    zeros = jnp.zeros((RIM, 128), WIDE)
    for local in heads:
        rate_sum = jnp.where(lane == first_head + local, rates[local], rate_sum)
        query, query_scale = queries[local]
        key, key_scale = keys[local]
        beta = betas[local]
        grad_query = carried * side_states[local][size:] + by_keys[local][size:]
        grad_key = (
            by_both[local]
            + last * to_exit[local]
            - beta * (by_keys[local][:size] + carried * side_states[local][:size])
        )
        grad_acts = (
            query_scale * (grad_query - query * jnp.sum(query * grad_query, axis=1, keepdims=True)),
            key_scale * (grad_key - key * jnp.sum(key * grad_key, axis=1, keepdims=True)),
            beta * grad_right[local],
        )
        for index in range(3):
            slot = 3 * local + index
            room = room_ref.at[slot]
            back = back_ref.at[slot]
            grad_conv = grad_acts[index] * kept[slot]
            weight = parts[index][0][:, lanes[local]].astype(WIDE)
            own = weight[0:1] * grad_conv
            edge_sum = zeros
            tap_ref[index, 0, 0:1, lanes[local]] = jnp.sum(
                grad_conv * room[pl.ds(RIM, size), :], axis=0, keepdims=True
            )
            for step in range(1, tap_count):
                masked = grad_conv * tap_masks[step - 1]
                tap_ref[index, 0, step : step + 1, lanes[local]] = jnp.sum(
                    masked * room[pl.ds(RIM - step, size), :], axis=0, keepdims=True
                )
                back[pl.ds(0, RIM), :] = zeros
                back[pl.ds(RIM, size), :] = weight[step : step + 1] * masked
                back[pl.ds(RIM + size, RIM), :] = zeros
                own = own + back[pl.ds(RIM + step, size), :]
                edge_sum = edge_sum + back[pl.ds(step, RIM), :]
            out_ref[index, 0, :, lanes[local]] = own.astype(LOW)
            edge_ref[index, 0, :, lanes[local]] = edge_sum
            tail_ref[index, 0, :, lanes[local]] = own[size - RIM :]
    rate_ref[0] = rate_sum * beta_all * (1.0 - beta_all)


def back_call(group, groups, cols, rows, beta, taps, rim, projected, solve, weights, state, exit_grad, grad):
    row_count, size, triple = projected.shape
    head_count = triple // (3 * 128)
    count = head_count // groups
    wide = count * 128
    tap_count = taps.shape[0]

    def of_row(block):
        return pl.BlockSpec(block, lambda r: (r, 0, 0))

    def part(rows_in, index):
        return pl.BlockSpec((1, rows_in, wide), lambda r: (r, 0, index * groups + group))

    def tap_part(index):
        return pl.BlockSpec((tap_count, wide), lambda r: (0, index * groups + group))

    def per_head(*block):
        return pl.BlockSpec((1, count) + block, lambda r: (r, group, 0, 0))

    def stacked(rows_in):
        return pl.BlockSpec((3, 1, rows_in, wide), lambda r: (0, r, 0, 0))

    def stacked_type(rows_in, kind):
        return jax.ShapeDtypeStruct((3, row_count, rows_in, wide), kind)

    return pl.pallas_call(
        functools.partial(back_kernel, group * count),
        grid=(row_count,),
        in_specs=[of_row((1,) + cols.shape[1:]), of_row((1,) + rows.shape[1:]), of_row((1,) + beta.shape[1:])]
        + [tap_part(i) for i in range(3)]
        + [part(RIM, i) for i in range(3)]
        + [part(size, i) for i in range(3)]
        + [per_head(size, size), per_head(size, 256), per_head(128, 128), per_head(128, 128), part(size, 0)],
        out_specs=[
            stacked(size), stacked(RIM), stacked(RIM), stacked(tap_count), of_row((1, size, 128)),
        ],
        out_shape=[
            stacked_type(size, LOW), stacked_type(RIM, WIDE), stacked_type(RIM, WIDE),
            stacked_type(tap_count, WIDE),
            jax.ShapeDtypeStruct((row_count, size, 128), WIDE),
        ],
        scratch_shapes=[
            pltpu.VMEM((3 * count, RIM + size, 128), WIDE),
            pltpu.VMEM((3 * count, size + 2 * RIM, 128), WIDE),
        ],
        compiler_params=pltpu.CompilerParams(vmem_limit_bytes=VMEM_BYTES),
        cost_estimate=timed(36 / groups),
        name="mixer_back",
    )(
        cols, rows, beta, taps, taps, taps, rim, rim, rim, projected, projected, projected,
        solve, weights, state, exit_grad, grad,
    )


def timed(microseconds):
    return pl.CostEstimate(
        flops=int(microseconds * 1.0e9), bytes_accessed=int(microseconds * 1.0e6), transcendentals=0
    )


def shifted(value, axis, steps):
    count = lax.axis_size(axis)
    leading, last = (max(0, -steps), min(count, count - steps))
    return lax.ppermute(value, axis, [(source, source + steps) for source in range(leading, last)])


def swap(value, bit):
    count = lax.axis_size("seq")
    return lax.ppermute(value, "seq", [(source, source ^ bit) for source in range(count)])


def put(outs, pieces, moves, position):
    for piece, parts in zip(pieces, moves):
        for member, relative, rows, start, source, count in parts:
            target = pl.multiple_of((position ^ relative) * rows + start, 16)
            outs[member][pl.ds(target, count), :] = piece[source : source + count, :]


def place_kernel(moves, position_ref, *refs):
    put(refs[len(moves) :], refs[: len(moves)], moves, position_ref[0])


def place(gathered):
    pieces, moves, sizes, position = gathered
    columns = pieces[0].shape[1]
    tile = next(size for size in (1408, 1024, 512, 256, 128) if columns % size == 0)
    return pl.pallas_call(
        functools.partial(place_kernel, moves),
        grid=(columns // tile,),
        in_specs=[pl.BlockSpec(memory_space=pltpu.SMEM)]
        + [pl.BlockSpec((piece.shape[0], tile), lambda j: (0, j)) for piece in pieces],
        out_specs=[pl.BlockSpec((size, tile), lambda j: (0, j)) for size in sizes],
        out_shape=[jax.ShapeDtypeStruct((size, columns), pieces[0].dtype) for size in sizes],
        compiler_params=pltpu.CompilerParams(vmem_limit_bytes=VMEM_BYTES),
        cost_estimate=timed(1 + sum(sizes) * columns / 1.2e6),
        name="place",
    )(position, *pieces)


def join(*values):
    return lax.optimization_barrier(values)


def gather_near(shard):
    return (swap(shard, 2), swap(shard, 4)) if seq_is_cube() else None


def gather_far(near):
    if not seq_is_cube():
        return None
    by_x, by_y = near
    half = by_x.shape[0] // 2
    return swap(by_x[:half], 4), swap(by_y[half:], 2)


def gather_core(shard, near, far):
    if not seq_is_cube():
        return [lax.all_gather(shard, "seq", axis=0)]
    mine = [shard, *near, *far]
    return mine + [swap(piece, 1) for piece in mine]


def placing(pieces, sizes):
    count = lax.axis_size("seq")
    if not seq_is_cube():
        parts, moves, offset = [], [], 0
        for member, size in enumerate(sizes):
            parts.append(pieces[0][:, offset : offset + size].reshape(count * size, -1))
            moves.append(((member, 0, 0, 0, 0, count * size),))
            offset += size
        return parts, tuple(moves), tuple(count * size for size in sizes), jnp.zeros((1,), jnp.int32)
    rows = sum(sizes)
    half = rows // 2
    spans = [(0, 0, rows), (2, 0, rows), (4, 0, rows), (6, 0, half), (6, half, half)]
    spans += [(relative ^ 1, first, span) for relative, first, span in spans]
    moves = []
    for relative, first, span in spans:
        parts, offset = [], 0
        for member, size in enumerate(sizes):
            low, high = max(first, offset), min(first + span, offset + size)
            if low < high:
                parts.append((member, relative, size, low - offset, low - first, high - low))
            offset += size
        moves.append(tuple(parts))
    position = lax.axis_index("seq").astype(jnp.int32).reshape(1)
    return pieces, tuple(moves), tuple(count * size for size in sizes), position


def project_kernel(
    moves, piece_count, position_ref, inputs_ref, valid_ref, bias_ref, *refs
):
    pieces, extra_pieces = refs[:piece_count], refs[piece_count : 2 * piece_count]
    joint_ref, extra_ref, normed_ref, out_ref, beta_ref, extras_ref = refs[2 * piece_count :]
    put([joint_ref], pieces, moves, position_ref[0])

    @pl.when(pl.program_id(0) == 0)
    def _():
        put([extra_ref], extra_pieces, moves, position_ref[0])
        extra = extra_ref[...]
        row = lax.broadcasted_iota(jnp.int32, (16, 128), 0)
        lane = lax.broadcasted_iota(jnp.int32, (16, 128), 1)
        extras = nt(jnp.where(lane == row + 8, 1.0, 0.0), extra)
        extras_ref[...] = extras
        inputs = inputs_ref[...].astype(WIDE)
        normed = (inputs * rms_scale(inputs) * extras[0:1]).astype(LOW)
        normed_ref[...] = normed
        beta_ref[...] = valid_ref[:, 0:1] * jax.nn.sigmoid(nn(normed, extra) + bias_ref[...])

    out_ref[...] = nn(normed_ref[...], joint_ref[...]).astype(LOW)


def project_call(gathered, inputs, valid, bias):
    pieces, moves, sizes, position = gathered
    tokens, width = inputs.shape
    columns = pieces[0].shape[1] - 128
    tile = 1024

    def whole(shape):
        return pl.BlockSpec(shape, lambda j: (0,) * len(shape))

    last = columns // 128
    return pl.pallas_call(
        functools.partial(project_kernel, moves, len(pieces)),
        grid=(columns // tile,),
        in_specs=[
            pl.BlockSpec(memory_space=pltpu.SMEM), whole((tokens, width)), whole(valid.shape), whole(bias.shape),
        ]
        + [pl.BlockSpec((piece.shape[0], tile), lambda j: (0, j)) for piece in pieces]
        + [pl.BlockSpec((piece.shape[0], 128), lambda j: (0, last)) for piece in pieces],
        out_specs=[
            pl.BlockSpec((width, tile), lambda j: (0, j)), whole((width, 128)), whole((tokens, width)),
            pl.BlockSpec((tokens, tile), lambda j: (0, j)), whole((tokens, 128)), whole((16, width)),
        ],
        out_shape=[
            jax.ShapeDtypeStruct((width, columns), LOW),
            jax.ShapeDtypeStruct((width, 128), LOW),
            jax.ShapeDtypeStruct((tokens, width), LOW),
            jax.ShapeDtypeStruct((tokens, columns), LOW),
            jax.ShapeDtypeStruct((tokens, 128), WIDE),
            jax.ShapeDtypeStruct((16, width), WIDE),
        ],
        compiler_params=pltpu.CompilerParams(vmem_limit_bytes=VMEM_BYTES),
        cost_estimate=timed(10),
        name="project",
    )(position, inputs, valid, bias, *pieces, *pieces)


def after(value, *earlier):
    return lax.optimization_barrier((value, earlier))[0]


def outer_turn_kernel(order_ref, left_ref, right_ref, out_ref, other_ref, own_ref, turned):
    rows = out_ref.shape[1]

    @pl.when(pl.program_id(0) == 0)
    def _():
        turned[...] = left_ref[...].T
        for index in range(4):
            first = pl.multiple_of(order_ref[index] * rows, 16)
            other_ref[index * rows : (index + 1) * rows, :] = turned[pl.ds(first, rows), :]
            second = pl.multiple_of(order_ref[4 + index] * rows, 16)
            own_ref[index * rows : (index + 1) * rows, :] = turned[pl.ds(second, rows), :]

    out_ref[...] = nn(other_ref[...], right_ref[0]).astype(LOW).reshape(out_ref.shape)


def outer_kernel(left_ref, right_ref, out_ref):
    out_ref[...] = nn(left_ref[...], right_ref[0]).astype(LOW).reshape(out_ref.shape)


def outer_add_kernel(left_ref, right_ref, add_ref, out_ref):
    total = nn(left_ref[...], right_ref[0])
    out_ref[...] = (
        (total + add_ref[...].reshape(total.shape).astype(WIDE)).astype(LOW).reshape(out_ref.shape)
    )


def outer_tile(parts, columns):
    sizes = (2816, 1024, 512, 256) if parts > 1 else (512, 256)
    return next(size for size in sizes if columns % size == 0)


def outer_specs(left_rows, right):
    parts, tokens, columns = right.shape
    rows = left_rows // 4
    tile = outer_tile(parts, columns)
    steps = columns // tile
    return dict(
        grid=(parts * steps,),
        left=pl.BlockSpec((left_rows, tokens), lambda j: (0, 0)),
        right=pl.BlockSpec((1, tokens, tile), lambda j: (j // steps, 0, j % steps)),
        out=pl.BlockSpec((4, rows, tile), lambda j: (0, 0, j)),
        out_type=jax.ShapeDtypeStruct((4, rows, parts * columns), LOW),
        params=pltpu.CompilerParams(vmem_limit_bytes=VMEM_BYTES),
        cost=timed(1 + tokens * left_rows * parts * columns / 1.8e8),
    )


def seq_is_cube():
    return lax.axis_size("seq") == 8


def outer_turn(left, right, position):
    tokens, features = left.shape
    if not seq_is_cube():
        return None, left, left
    specs = outer_specs(features // 2, right)
    order = position ^ jnp.array([1, 3, 5, 7, 0, 2, 4, 6], jnp.int32)
    left_type = jax.ShapeDtypeStruct((features // 2, tokens), LOW)
    return pl.pallas_call(
        outer_turn_kernel,
        grid=specs["grid"],
        in_specs=[
            pl.BlockSpec(memory_space=pltpu.SMEM),
            pl.BlockSpec((tokens, features), lambda j: (0, 0)),
            specs["right"],
        ],
        out_specs=[specs["out"], specs["left"], specs["left"]],
        out_shape=[specs["out_type"], left_type, left_type],
        scratch_shapes=[pltpu.VMEM((features, tokens), LOW)],
        compiler_params=specs["params"],
        cost_estimate=specs["cost"],
        name="outer_turn",
    )(order, left, right)


def outer(left, right):
    if not seq_is_cube():
        return None
    specs = outer_specs(left.shape[0], right)
    return pl.pallas_call(
        outer_kernel,
        grid=specs["grid"],
        in_specs=[specs["left"], specs["right"]],
        out_specs=specs["out"],
        out_shape=specs["out_type"],
        compiler_params=specs["params"],
        cost_estimate=specs["cost"],
        name="outer",
    )(left, right)


def outer_add(left, right, received):
    if not seq_is_cube():
        full = [jnp.einsum("td,te->de", left, right[i], preferred_element_type=WIDE) for i in range(right.shape[0])]
        full = jnp.concatenate(full, axis=-1).astype(LOW)
        return lax.psum_scatter(full, "seq", scatter_dimension=0, tiled=True)
    specs = outer_specs(left.shape[0], right)
    return pl.pallas_call(
        outer_add_kernel,
        grid=specs["grid"],
        in_specs=[specs["left"], specs["right"], specs["out"]],
        out_specs=specs["out"],
        out_shape=specs["out_type"],
        compiler_params=specs["params"],
        cost_estimate=specs["cost"],
        name="outer_add",
    )(left, right, received)


def send_other(other):
    return swap(other, 1) if seq_is_cube() else None


def scatter_far(own):
    if not seq_is_cube():
        return own
    half = own.shape[1] // 2
    return own, swap(own[3, :half], 2), swap(own[3, half:], 4)


def scatter_near(stage):
    if not seq_is_cube():
        return stage
    own, to_second, to_first = stage
    half = own.shape[1] // 2
    first = jnp.concatenate(
        [own[1, :half], (own[1, half:].astype(WIDE) + to_first.astype(WIDE)).astype(LOW)], axis=0
    )
    second = jnp.concatenate(
        [(own[2, :half].astype(WIDE) + to_second.astype(WIDE)).astype(LOW), own[2, half:]], axis=0
    )
    return own[0], swap(first, 2), swap(second, 4)


def scatter_end(stage):
    if not seq_is_cube():
        return stage
    own, by_x, by_y = stage
    return (own.astype(WIDE) + by_x.astype(WIDE) + by_y.astype(WIDE)).astype(LOW)


def rows_are_line():
    return lax.axis_size("row") == 4


def row_inward(value):
    if not rows_are_line():
        return lax.psum(value, "row")
    return value, lax.ppermute(value, "row", [(0, 1), (3, 2)])


def row_across(stage):
    if not rows_are_line():
        return stage
    value, received = stage
    value = (value.astype(WIDE) + received.astype(WIDE)).astype(value.dtype)
    return value, lax.ppermute(value, "row", [(1, 2), (2, 1)])


def row_outward(stage):
    if not rows_are_line():
        return stage
    value, received = stage
    value = (value.astype(WIDE) + received.astype(WIDE)).astype(value.dtype)
    return value, lax.ppermute(value, "row", [(1, 0), (2, 3)])


def row_end(stage):
    if not rows_are_line():
        return stage.astype(WIDE)
    value, received = stage
    index = lax.axis_index("row")
    return jnp.where((index == 0) | (index == 3), received, value).astype(WIDE)


def bias_rows(value):
    if not seq_is_cube():
        return lax.psum(value, ("seq", "row"))
    return row_end(row_outward(row_across(row_inward(value))))


def on_device(
    inputs,
    lengths,
    norm_gain,
    w_qkv,
    w_beta,
    beta_bias,
    w_conv,
    w_out,
    ffn_gain,
    w_gate,
    w_up,
    w_down,
    cotangent,
):
    row_count, slot_count, width = inputs.shape
    token_count = row_count * slot_count
    head_count = beta_bias.shape[0]
    tap_count = w_conv.shape[0]
    rim_size = tap_count - 1
    pairs = row_count * head_count
    shard = norm_gain.shape[0]
    seq_count = lax.axis_size("seq")
    position = lax.axis_index("seq").astype(jnp.int32)

    by_lane = jnp.transpose(w_conv.reshape(tap_count, 3, shard), (2, 0, 1)).reshape(shard, -1)
    extra = jnp.concatenate([w_beta, norm_gain[:, None], ffn_gain[:, None], by_lane], axis=1)
    extra = jnp.pad(extra, ((0, 0), (0, 128 - extra.shape[1])))
    w_joint = jnp.concatenate([w_qkv, extra], axis=1)
    joint_near = gather_near(w_joint)
    doc_ends = jnp.cumsum(lengths, axis=1, dtype=jnp.int32)
    spots = position * slot_count - rim_size + jnp.arange(slot_count + rim_size, dtype=jnp.int32)
    ext_docs = jnp.sum(
        (spots[None, :, None] >= doc_ends[:, None, :]).astype(jnp.int32), axis=2, dtype=jnp.int32
    )
    ext_docs = jnp.where(spots[None, :] < 0, -1, ext_docs)
    own_docs = ext_docs[:, rim_size:]
    valid_mask = (spots[None, rim_size:] < doc_ends[:, -1:]).astype(WIDE)
    shown = [own_docs.astype(WIDE)]
    for offset in range(1, tap_count):
        before = ext_docs[:, rim_size - offset : rim_size - offset + slot_count]
        shown.append((before == own_docs).astype(WIDE))
    shown.append((own_docs == ext_docs[:, rim_size - 1 : rim_size]).astype(WIDE))
    shown.append((own_docs == own_docs[:, -1:]).astype(WIDE))
    shown += [valid_mask, valid_mask]
    cols = jnp.stack(shown, axis=-1)
    valid = jnp.broadcast_to(valid_mask.reshape(token_count, 1), (token_count, 8))
    rows = jnp.broadcast_to(own_docs.astype(WIDE)[:, None, :], (row_count, 8, slot_count))
    bounds = jnp.arange(seq_count, dtype=jnp.int32) * slot_count
    doc_first = jnp.sum((bounds[None, :, None] - 1 >= doc_ends[:, None, :]).astype(jnp.int32), axis=2)
    doc_last = jnp.sum(
        (bounds[None, :, None] + slot_count - 1 >= doc_ends[:, None, :]).astype(jnp.int32), axis=2
    )
    keep = (doc_first == doc_last).astype(WIDE)
    share = -(-pairs // seq_count)
    keep_pairs = jnp.pad(
        jnp.repeat(keep, head_count, axis=0), ((0, share * seq_count - pairs), (0, 0))
    )
    keep_own = lax.dynamic_slice_in_dim(keep_pairs, position * share, share, axis=0)

    joint_near, cols, rows, valid, keep_own = join(joint_near, cols, rows, valid, keep_own)
    joint_far = gather_far(joint_near)
    joint_pieces = placing(gather_core(w_joint, joint_near, joint_far), (shard,))
    gate_near = gather_near(after(w_gate, joint_far))

    tokens_in = inputs.reshape(token_count, width)
    bias_row = jnp.pad(beta_bias.astype(WIDE), (0, 128 - head_count))[None]
    joint, joint_extra, normed, projected, beta, extras = project_call(
        joint_pieces, tokens_in, valid, bias_row
    )
    first_gain, second_gain = extras[0:1], extras[1:2]
    taps = extras[2 : 2 + 3 * tap_count].reshape(tap_count, 3, seq_count, shard)
    taps = jnp.swapaxes(taps, 1, 2).reshape(tap_count, 3 * width).astype(LOW)
    projected = projected.reshape(row_count, slot_count, 3 * width)
    beta = beta.reshape(row_count, slot_count, 128)
    rim = shifted(projected[:, slot_count - RIM :], "seq", 1)

    rim, projected, gate_near = join(rim, projected, gate_near)
    gate_far = gather_far(gate_near)
    up_near = gather_near(after(w_up, gate_near))
    eff, local_out, maps, solve, weights = prepare_call(cols, rows, beta, taps, rim, projected)
    maps, gate_far, up_near = join(maps, gate_far, up_near)
    maps_here = exchange(maps.reshape((pairs,) + maps.shape[2:]), seq_count)
    gate_pieces = placing(gather_core(w_gate, gate_near, gate_far), (shard,))
    up_far = gather_far(up_near)
    out_near = gather_near(after(w_out, up_near))
    maps_here, up_far, out_near = join(maps_here, up_far, out_near)
    states_here = chain_call(chain_forward_kernel, keep_own, maps_here)
    down_near = gather_near(after(w_down, states_here))
    state = to_home(states_here, pairs).reshape((row_count, head_count, 128, 128))
    out_far = gather_far(after(out_near, states_here))
    up_pieces = placing(gather_core(w_up, up_near, after(up_far, states_here)), (shard,))
    state, out_far, down_near = join(state, out_far, down_near)
    down_far = gather_far(down_near)
    (full_out,) = place(placing(gather_core(w_out, out_near, out_far), (shard,)))
    down_pieces = gather_core(w_down, down_near, after(down_far, full_out))
    (full_down,) = place(placing(down_pieces, (w_down.shape[0],)))

    (
        heads_low, second, act, grad_pair, output, upstream_low,
        grad_hidden, grad_mix_low, grad_heads, local_grad, grad_ffn_gain,
    ) = feed_call(
        eff, local_out, state, tokens_in, cotangent.reshape(token_count, width), valid, second_gain,
        full_out, gate_pieces, up_pieces, full_down,
    )
    grad_heads = grad_heads.reshape(row_count, slot_count, width)

    grads_here = exchange(local_grad.reshape((pairs, 128, 128)), seq_count)
    other_pair, _, left_pair = outer_turn(second, grad_pair, position)
    grads_here, left_pair = join(grads_here, left_pair)
    from_pair = send_other(other_pair)
    exits_here = chain_call(chain_backward_kernel, keep_own, maps_here, grads_here)
    exit_grad = to_home(exits_here, pairs).reshape((row_count, head_count, 128, 128))
    other_down, _, left_down = outer_turn(after(act, exits_here), upstream_low[None], position)
    from_down = send_other(other_down)
    own_pair = outer_add(after(left_pair, left_down), grad_pair, from_pair)
    exit_grad, own_pair = join(exit_grad, own_pair)
    far_pair = scatter_far(own_pair)

    def pull(group, exit_grad):
        grad_parts, edges, tails, tap_sums, logits = back_call(
            group, 2, cols, rows, beta, taps, rim, projected, solve, weights, state, exit_grad, grad_heads
        )
        return grad_parts, shifted(edges.astype(LOW), "seq", -1), tails, jnp.sum(tap_sums, axis=1), logits

    def fix(grad_parts, back_rim, tails):
        fixed = lax.dynamic_update_slice(
            grad_parts, (tails + back_rim.astype(WIDE)).astype(LOW), (0, 0, slot_count - RIM, 0)
        )
        return fixed.reshape(3, token_count, -1)

    first_parts, first_rim, first_tails, first_taps, first_logits = pull(0, exit_grad)
    far_pair, first_logits, from_down = join(far_pair, first_logits, from_down)
    own_down = outer_add(after(left_down, first_logits), upstream_low[None], from_down)
    first_rim, own_down, first_parts = join(first_rim, own_down, first_parts)
    near_pair = scatter_near(after(far_pair, own_down))
    first_grad = fix(first_parts, first_rim, first_tails)
    other_first, left_other, left_own = outer_turn(normed, first_grad, position)
    from_first = send_other(other_first)
    other_out, _, left_out = outer_turn(after(heads_low, left_own), grad_mix_low[None], position)
    from_out = send_other(other_out)
    second_parts, second_rim, second_tails, second_taps, second_logits = pull(1, after(exit_grad, left_out))
    near_pair, from_first, from_out, second_logits = join(near_pair, from_first, from_out, second_logits)
    shard_pair = scatter_end(near_pair)
    pair = row_inward(shard_pair)
    far_down = scatter_far(after(own_down, second_logits))
    own_first = outer_add(after(left_own, second_logits, shard_pair), first_grad, from_first)
    own_out = outer_add(after(left_out, own_first), grad_mix_low[None], from_out)
    second_rim, own_out, second_parts, own_first = join(second_rim, own_out, second_parts, own_first)
    far_first = scatter_far(own_first)
    second_grad = fix(second_parts, second_rim, second_tails)
    other_second = outer(after(left_other, own_out), second_grad)
    other_second, far_first, far_down, own_out = join(other_second, far_first, far_down, own_out)
    from_second = send_other(other_second)
    near_first = scatter_near(far_first)
    near_down = scatter_near(far_down)
    far_out = scatter_far(own_out)

    grad_logits = (first_logits + second_logits).reshape(token_count, 128)
    grad_inputs, grad_norm_gain = project_back_call(
        first_grad, after(second_grad, other_second), joint, grad_logits, joint_extra, tokens_in, first_gain, grad_hidden
    )
    grad_beta_w = jnp.einsum(
        "td,th->dh", normed.astype(WIDE), grad_logits[:, :head_count], precision=lax.Precision.HIGHEST
    )
    grad_conv_w = jnp.stack([first_taps, second_taps], axis=2)
    grad_conv_w = jnp.swapaxes(grad_conv_w, 0, 1).reshape(tap_count, seq_count, 3, shard)
    minor = jnp.concatenate(
        [
            grad_beta_w.reshape(seq_count, shard, head_count),
            grad_norm_gain.reshape(seq_count, shard, 1),
            grad_ffn_gain.reshape(seq_count, shard, 1),
            jnp.transpose(grad_conv_w, (1, 3, 0, 2)).reshape(seq_count, shard, 3 * tap_count),
        ],
        axis=2,
    )
    minor = jnp.pad(minor, ((0, 0), (0, 0), (0, 128 - minor.shape[2])))
    if seq_is_cube():
        order = position ^ jnp.array([1, 3, 5, 7, 0, 2, 4, 6], jnp.int32)
        minor = jnp.take(minor, order, axis=0)
        own_minor = (minor[4:] + swap(minor[:4].astype(LOW), 1).astype(WIDE)).astype(LOW)
    else:
        own_minor = lax.psum_scatter(
            minor.reshape(width, 128).astype(LOW), "seq", scatter_dimension=0, tiled=True
        )
    from_second, grad_inputs, near_first, far_out, own_minor, grad_logits, pair = join(
        from_second, grad_inputs, near_first, far_out, own_minor, grad_logits, pair
    )
    pair = row_across(pair)
    first = row_inward(scatter_end(near_first))
    near_out = scatter_near(far_out)
    own_second = jnp.concatenate(
        [outer_add(left_own, second_grad, from_second), own_minor], axis=-1
    )
    far_second = scatter_far(own_second)
    far_second, near_down, near_out, first = join(far_second, near_down, near_out, first)
    near_second = scatter_near(far_second)
    down = row_inward(scatter_end(near_down))
    out = row_inward(scatter_end(near_out))
    first = row_across(first)
    bias = jnp.sum(grad_logits, axis=0, keepdims=True)
    if seq_is_cube():
        bias = bias + swap(bias, 1)
    near_second, first, down, out, bias, pair = join(near_second, first, down, out, bias, pair)
    pair = row_outward(pair)
    second_ = row_inward(scatter_end(near_second))
    first = row_outward(first)
    down = row_across(down)
    out = row_across(out)
    if seq_is_cube():
        bias = bias + swap(bias, 2)
    second_, first, down, out, bias = join(second_, first, down, out, bias)
    second_ = row_across(second_)
    down = row_outward(down)
    out = row_outward(out)
    if seq_is_cube():
        bias = bias + swap(bias, 4)
    second_, down, out, bias = join(second_, down, out, bias)
    second_ = row_outward(second_)
    bias = bias_rows(bias)
    second_, pair, first, down, out = join(second_, pair, first, down, out)
    total_first, total_second, total_down, total_out = (row_end(value) for value in (first, second_, down, out))
    total_pair = row_end(pair)
    bias_total = bias[0, :head_count]
    half = width // 2
    total_qkv = jnp.concatenate(
        [
            total[:, part * half : (part + 1) * half]
            for part in range(3)
            for total in (total_first, total_second)
        ],
        axis=1,
    )
    small = total_second[:, 3 * half :]
    columns = head_count + 2
    total_conv = jnp.transpose(
        small[:, columns : columns + 3 * tap_count].reshape(shard, tap_count, 3), (1, 2, 0)
    ).reshape(tap_count, -1)
    units = w_gate.shape[1]
    return (
        output.reshape(inputs.shape),
        grad_inputs.reshape(inputs.shape),
        small[:, head_count],
        total_qkv,
        small[:, :head_count],
        bias_total,
        total_conv,
        total_out,
        small[:, head_count + 1],
        total_pair[:, :units],
        total_pair[:, units:],
        total_down,
    )


def solution(mesh):
    placed = (
        P("row", "seq", None),
        P("row", None),
        P("seq"),
        P("seq", None),
        P("seq", None),
        P(),
        P(None, "seq"),
        P("seq", None),
        P("seq"),
        P("seq", None),
        P("seq", None),
        P("seq", None),
        P("row", "seq", None),
    )
    return jax.shard_map(
        on_device,
        mesh=mesh,
        in_specs=placed,
        out_specs=(
            P("row", "seq", None),
            P("row", "seq", None),
            P("seq"),
            P("seq", None),
            P("seq", None),
            P(),
            P(None, "seq"),
            P("seq", None),
            P("seq"),
            P("seq", None),
            P("seq", None),
            P("seq", None),
        ),
        check_vma=False,
    )
```

```python
import functools

import jax
import jax.numpy as jnp
from jax import lax
from jax.experimental import pallas as pl
from jax.experimental.pallas import tpu as pltpu
from jax.sharding import PartitionSpec as P

EPSILON = 1e-06
LOW = jnp.bfloat16
WIDE = jnp.float32
HEADS_STEP = 8
RIM = 8
VMEM_BYTES = 56 * 1024 * 1024


def nn(left, right):
    return lax.dot_general(
        left.astype(LOW), right.astype(LOW), (((1,), (0,)), ((), ())), preferred_element_type=WIDE
    )


def nt(left, right):
    return lax.dot_general(
        left.astype(LOW), right.astype(LOW), (((1,), (1,)), ((), ())), preferred_element_type=WIDE
    )


def tn(left, right):
    return lax.dot_general(
        left.astype(LOW), right.astype(LOW), (((0,), (0,)), ((), ())), preferred_element_type=WIDE
    )


def split(value):
    high = value.astype(LOW)
    return high, (value - high.astype(WIDE)).astype(LOW)


def nn_fine(left, right):
    left_high, left_low = split(left)
    right_high, right_low = split(right)
    return nn(left_high, right_high) + nn(left_high, right_low) + nn(left_low, right_high)


def call_after(ready, kernel, in_specs, **settings):
    ready = jax.tree.leaves(ready)

    def run(*refs):
        kernel(*refs[len(ready) :])

    made = pl.pallas_call(
        run, in_specs=[pl.BlockSpec(memory_space=pl.ANY) for _ in ready] + list(in_specs), **settings
    )
    return lambda *arrays: made(*ready, *arrays)


def rms_scale(values):
    return lax.rsqrt(jnp.mean(values * values, axis=-1, keepdims=True) + EPSILON)


def windows_of(rim, block, taps, room):
    size = block.shape[0]
    room[pl.ds(0, RIM), :] = rim
    room[pl.ds(RIM, size), :] = block
    return [block] + [room[pl.ds(RIM - step, size), :] for step in range(1, taps)]


def convolve(windows, weights, tap_masks):
    total = weights[0:1] * windows[0]
    for step in range(1, len(windows)):
        total = total + weights[step : step + 1] * (windows[step] * tap_masks[step - 1])
    return total


def pair_distance(size):
    row = lax.broadcasted_iota(jnp.int32, (size, size), 0)
    column = lax.broadcasted_iota(jnp.int32, (size, size), 1)
    return row, column


def inverse_unit_lower(stricts, corners):
    size = stricts[0].shape[0]
    row, column = pair_distance(size)
    eye = (row == column).astype(WIDE)
    results = [eye - strict * corners[0] for strict in stricts]
    level = 1
    while (1 << level) < size:
        lows = [result.astype(LOW) for result in results]
        halves = [
            nn((strict * corners[level]).astype(LOW), low).astype(LOW)
            for strict, low in zip(stricts, lows)
        ]
        results = [
            result - nn(low, half) for result, low, half in zip(results, lows, halves)
        ]
        level += 1
    if REFINE:
        rests = []
        for strict, result in zip(stricts, results):
            high, low = split(result)
            strict_high, strict_low = split(strict)
            rests.append(
                eye - result - nn(strict_high, high) - nn(strict_high, low) - nn(strict_low, high)
            )
        results = [result + nn(result, rest) for result, rest in zip(results, rests)]
    return results


REFINE = True


def unit_and_scale(values):
    scale = lax.rsqrt(jnp.sum(values * values, axis=-1, keepdims=True) + EPSILON)
    return values * scale, scale


def head_masks(cols, rows):
    doc_col, doc_row = cols[:, 0:1], rows[0:1, :]
    size = cols.shape[0]
    row, column = pair_distance(size)
    same = doc_col == doc_row
    inclusive = same & (row >= column)
    strict = same & (row > column)
    tap_masks = [cols[:, 1:2], cols[:, 2:3], cols[:, 3:4]]
    return row, column, inclusive, strict, tap_masks, cols[:, 4:5], cols[:, 5:6]


def pick_head(table, head):
    lane = lax.broadcasted_iota(jnp.int32, table.shape, 1)
    return jnp.sum(jnp.where(lane == head, table, 0.0), axis=1, keepdims=True)


def prepare_kernel(
    cols_ref, rows_ref, beta_ref, taps_q, taps_k, taps_v, rim_q, rim_k, rim_v, in_q, in_k, in_v,
    eff_ref, local_ref, maps_ref, solve_ref, weights_ref, room_ref,
):
    cols, rows = cols_ref[0], rows_ref[0]
    row, column, inclusive, strict, tap_masks, carried, last = head_masks(cols, rows)
    beta_all = beta_ref[0]
    tap_count = taps_q.shape[0]
    size = cols.shape[0]
    half = size // 2
    apart = (row ^ column)[:half, :half]
    corners = []
    level = 0
    while (1 << level) < half:
        corners.append(((apart >> level) == 1).astype(WIDE))
        level += 1
    heads = range(HEADS_STEP)
    lanes = [slice(local * 128, (local + 1) * 128) for local in heads]
    queries, keys, values, betas = [], [], [], []
    for local in heads:
        acts = []
        for index, (taps, rim, block) in enumerate(
            ((taps_q, rim_q, in_q), (taps_k, rim_k, in_k), (taps_v, rim_v, in_v))
        ):
            windows = windows_of(
                rim[0, :, lanes[local]].astype(WIDE),
                block[0, :, lanes[local]].astype(WIDE),
                tap_count,
                room_ref.at[3 * local + index],
            )
            acts.append(jax.nn.silu(convolve(windows, taps[:, lanes[local]].astype(WIDE), tap_masks)))
        queries.append(unit_and_scale(acts[0])[0])
        keys.append(unit_and_scale(acts[1])[0])
        values.append(acts[2])
        betas.append(pick_head(beta_all, pl.program_id(1) * HEADS_STEP + local))
    grams = [
        nt(jnp.concatenate([key.astype(LOW), query.astype(LOW)], axis=0), key)
        for key, query in zip(keys, queries)
    ]
    systems = [jnp.where(strict, gram[:size] * beta, 0.0) for gram, beta in zip(grams, betas)]
    scores = [jnp.where(inclusive, gram[size:], 0.0).astype(LOW) for gram in grams]
    blocks = inverse_unit_lower(
        [system[:half, :half] for system in systems] + [system[half:, half:] for system in systems],
        corners,
    )
    upper = [block.astype(LOW) for block in blocks[:HEADS_STEP]]
    lower = [block.astype(LOW) for block in blocks[HEADS_STEP:]]
    crossing = [nn(system[half:, :half], block) for system, block in zip(systems, upper)]
    crossing = [-nn(block, cross) for block, cross in zip(lower, crossing)]
    solves = [
        jnp.concatenate(
            [
                jnp.concatenate([first, jnp.zeros((half, half), LOW)], axis=1),
                jnp.concatenate([cross.astype(LOW), second], axis=1),
            ],
            axis=0,
        )
        for first, second, cross in zip(upper, lower, crossing)
    ]
    rights = [
        jnp.concatenate([(beta * carried) * key, beta * value], axis=1)
        for beta, key, value in zip(betas, keys, values)
    ]
    weights = [nn(solve, right).astype(LOW) for solve, right in zip(solves, rights)]
    mixed = [nn(score, weight) for score, weight in zip(scores, weights)]
    maps = [tn(last * key, weight) for key, weight in zip(keys, weights)]
    for local in heads:
        eff_ref[0, local] = (carried * queries[local] - mixed[local][:, :128]).astype(LOW)
        local_ref[0, :, lanes[local]] = mixed[local][:, 128:]
        maps_ref[0, local] = maps[local].astype(LOW)
        solve_ref[0, local] = solves[local]
        weights_ref[0, local] = weights[local]


def prepare_call(cols, rows, beta, taps, rim, projected):
    row_count, size, triple = projected.shape
    head_count = triple // (3 * 128)
    groups = head_count // HEADS_STEP
    wide = HEADS_STEP * 128
    tap_count = taps.shape[0]

    def of_row(block):
        return pl.BlockSpec(block, lambda r, g: (r, 0, 0))

    def part(rows_in, index):
        return pl.BlockSpec((1, rows_in, wide), lambda r, g: (r, 0, index * groups + g))

    def tap_part(index):
        return pl.BlockSpec((tap_count, wide), lambda r, g: (0, index * groups + g))

    def per_head(*block):
        return pl.BlockSpec((1, HEADS_STEP) + block, lambda r, g: (r, g, 0, 0))

    return pl.pallas_call(
        prepare_kernel,
        grid=(row_count, groups),
        in_specs=[of_row((1,) + cols.shape[1:]), of_row((1,) + rows.shape[1:]), of_row((1,) + beta.shape[1:])]
        + [tap_part(i) for i in range(3)]
        + [part(RIM, i) for i in range(3)]
        + [part(size, i) for i in range(3)],
        out_specs=[
            per_head(size, 128),
            pl.BlockSpec((1, size, wide), lambda r, g: (r, 0, g)),
            per_head(128, 256),
            per_head(size, size),
            per_head(size, 256),
        ],
        out_shape=[
            jax.ShapeDtypeStruct((row_count, head_count, size, 128), LOW),
            jax.ShapeDtypeStruct((row_count, size, head_count * 128), WIDE),
            jax.ShapeDtypeStruct((row_count, head_count, 128, 256), LOW),
            jax.ShapeDtypeStruct((row_count, head_count, size, size), LOW),
            jax.ShapeDtypeStruct((row_count, head_count, size, 256), LOW),
        ],
        scratch_shapes=[pltpu.VMEM((3 * HEADS_STEP, RIM + size, 128), WIDE)],
        compiler_params=pltpu.CompilerParams(vmem_limit_bytes=VMEM_BYTES),
        cost_estimate=timed(22),
        name="prepare",
    )(cols, rows, beta, taps, taps, taps, rim, rim, rim, projected, projected, projected)


def chain_forward_kernel(keep_ref, maps_ref, out_ref):
    count, pairs = maps_ref.shape[0], maps_ref.shape[1]
    states = [jnp.zeros((128, 128), WIDE) for _ in range(pairs)]
    for device in range(count):
        for pair in range(pairs):
            state = states[pair]
            out_ref[device, pair] = state.astype(LOW)
            decay = maps_ref[device, pair, :, :128]
            write = maps_ref[device, pair, :, 128:]
            states[pair] = (
                keep_ref[pair, device] * state - nn(decay, state) + write.astype(WIDE)
            )


def chain_backward_kernel(keep_ref, maps_ref, grads_ref, out_ref):
    count, pairs = maps_ref.shape[0], maps_ref.shape[1]
    states = [jnp.zeros((128, 128), WIDE) for _ in range(pairs)]
    for device in reversed(range(count)):
        for pair in range(pairs):
            state = states[pair]
            out_ref[device, pair] = state.astype(LOW)
            decay = maps_ref[device, pair, :, :128]
            states[pair] = (
                keep_ref[pair, device] * state
                - tn(decay, state)
                + grads_ref[device, pair].astype(WIDE)
            )


def chain_call(kernel, keep, *arrays, ready=()):
    count, pairs = arrays[0].shape[:2]
    return call_after(
        ready,
        kernel,
        in_specs=[pl.BlockSpec(memory_space=pltpu.SMEM)]
        + [pl.BlockSpec(memory_space=pltpu.VMEM) for _ in arrays],
        out_specs=pl.BlockSpec(memory_space=pltpu.VMEM),
        out_shape=jax.ShapeDtypeStruct((count, pairs, 128, 128), LOW),
        compiler_params=pltpu.CompilerParams(vmem_limit_bytes=VMEM_BYTES),
        cost_estimate=timed(3),
        name="chain",
    )(keep, *arrays)


def exchange(value, count):
    pairs = value.shape[0]
    share = -(-pairs // count)
    padded = jnp.pad(value, ((0, share * count - pairs),) + ((0, 0),) * (value.ndim - 1))
    cut = padded.reshape((count, share) + value.shape[1:])
    return lax.all_to_all(cut, "seq", split_axis=0, concat_axis=0)


def to_home(value, pairs):
    moved = lax.all_to_all(value, "seq", split_axis=0, concat_axis=0)
    return moved.reshape((-1,) + value.shape[2:])[:pairs]


def feed_kernel(
    gate_moves, up_moves, position_ref, eff_ref, local_ref, state_ref, inputs_ref, cot_ref, valid_ref, gain_ref, w_out_ref,
    down_ref, *refs,
):
    count = len(gate_moves)
    (
    heads_ref, second_ref, act_ref, pair_ref, output_ref, upstream_ref,
    hidden_grad_ref, mix_ref, heads_grad_ref, local_grad_ref, gain_grad_ref,
    hidden_ref, out_sum, second_sum, gate_ref, up_ref,
    ) = refs[count + len(up_moves) :]
    put([gate_ref], refs[:count], gate_moves, position_ref[0])
    put([up_ref], refs[count : count + len(up_moves)], up_moves, position_ref[0])
    step, last_step = pl.program_id(0), pl.num_programs(0) - 1
    row_count, head_count, size = eff_ref.shape[:3]

    @pl.when(step == 0)
    def _():
        for r in range(row_count):
            tokens = slice(r * size, (r + 1) * size)
            for h in range(head_count):
                lanes = slice(h * 128, (h + 1) * 128)
                heads_ref[tokens, lanes] = (
                    local_ref[r, :, lanes] + nn(eff_ref[r, h], state_ref[r, h])
                ).astype(LOW)
        hidden = inputs_ref[...].astype(WIDE) + nn(heads_ref[...], w_out_ref[...])
        hidden_ref[...] = hidden
        second_ref[...] = (hidden * rms_scale(hidden) * gain_ref[...]).astype(LOW)
        upstream_ref[...] = (cot_ref[...].astype(WIDE) * valid_ref[:, 0:1]).astype(LOW)
        out_sum[...] = hidden
        second_sum[...] = jnp.zeros(second_sum.shape, WIDE)

    second = second_ref[...]
    gated = nn(second, gate_ref[...])
    lifted = nn(second, up_ref[...])
    grad_act = nt(upstream_ref[...], down_ref[...])
    gate = jax.nn.sigmoid(gated)
    opened = gated * gate
    act = (opened * lifted).astype(LOW)
    act_ref[...] = act
    grad_gated = (grad_act * lifted * gate * (1.0 + gated * (1.0 - gate))).astype(LOW)
    grad_lifted = (grad_act * opened).astype(LOW)
    pair_ref[0] = grad_gated
    pair_ref[1] = grad_lifted
    out_sum[...] += nn(act, down_ref[...])
    second_sum[...] += nt(grad_gated, gate_ref[...]) + nt(grad_lifted, up_ref[...])

    @pl.when(step == last_step)
    def _():
        output_ref[...] = (valid_ref[:, 0:1] * out_sum[...]).astype(LOW)
        hidden = hidden_ref[...]
        scale = rms_scale(hidden)
        grad_second = second_sum[...]
        gain_grad_ref[...] = jnp.sum(grad_second * hidden * scale, axis=0, keepdims=True)
        scaled = gain_ref[...] * grad_second
        grad_hidden = (
            upstream_ref[...].astype(WIDE)
            + scale * scaled
            - hidden * (scale * scale * scale * jnp.mean(scaled * hidden, axis=-1, keepdims=True))
        )
        hidden_grad_ref[...] = grad_hidden
        mix_ref[...] = grad_hidden.astype(LOW)
        heads_grad_ref[...] = nt(mix_ref[...], w_out_ref[...]).astype(LOW)
        for r in range(row_count):
            tokens = slice(r * size, (r + 1) * size)
            for h in range(head_count):
                lanes = slice(h * 128, (h + 1) * 128)
                local_grad_ref[r, h] = tn(eff_ref[r, h], heads_grad_ref[tokens, lanes]).astype(LOW)


def feed_call(eff, local, state, inputs, cot, valid, gain, w_out, gate, up, w_down):
    row_count, head_count, size = eff.shape[:3]
    tokens, width = inputs.shape
    pieces, position = gate[0] + up[0], gate[3]
    units = pieces[0].shape[1]
    tile = FEED_TILE

    def whole(shape):
        return pl.BlockSpec(shape, lambda j: (0,) * len(shape), pipeline_mode=pl.Buffered(1))

    token_low = jax.ShapeDtypeStruct((tokens, width), LOW)
    token_spec = whole((tokens, width))
    return pl.pallas_call(
        functools.partial(feed_kernel, gate[1], up[1]),
        grid=(units // tile,),
        in_specs=[
            pl.BlockSpec(memory_space=pltpu.SMEM), whole(eff.shape), whole(local.shape), whole(state.shape), token_spec, token_spec,
            whole(valid.shape), whole(gain.shape), whole(w_out.shape),
            pl.BlockSpec((tile, width), lambda j: (j, 0)),
        ]
        + [pl.BlockSpec((piece.shape[0], tile), lambda j: (0, j)) for piece in pieces],
        out_specs=[
            token_spec, token_spec,
            pl.BlockSpec((tokens, tile), lambda j: (0, j)),
            pl.BlockSpec((2, tokens, tile), lambda j: (0, 0, j)),
            token_spec, token_spec, token_spec, token_spec, token_spec,
            whole(state.shape), whole((1, width)),
        ],
        out_shape=[
            token_low, token_low,
            jax.ShapeDtypeStruct((tokens, units), LOW),
            jax.ShapeDtypeStruct((2, tokens, units), LOW),
            token_low, token_low,
            jax.ShapeDtypeStruct((tokens, width), WIDE),
            token_low, token_low,
            jax.ShapeDtypeStruct(state.shape, LOW),
            jax.ShapeDtypeStruct((1, width), WIDE),
        ],
        scratch_shapes=[pltpu.VMEM((tokens, width), WIDE)] * 3 + [pltpu.VMEM((width, tile), LOW)] * 2,
        compiler_params=pltpu.CompilerParams(vmem_limit_bytes=VMEM_BYTES),
        cost_estimate=timed(38),
        name="feed",
    )(position, eff, local, state, inputs, cot, valid, gain, w_out, w_down, *pieces)


FEED_TILE = 256


def project_back_kernel(
    first_ref, second_ref, weight_ref, logit_ref, extra_ref, inputs_ref, gain_ref, hidden_grad_ref,
    out_ref, gain_grad_ref, total,
):
    step = pl.program_id(0)
    half = first_ref.shape[2]

    @pl.when(step == 0)
    def _():
        high, low = split(logit_ref[...])
        total[...] = nt(high, extra_ref[...]) + nt(low, extra_ref[...])

    total[...] += nt(first_ref[0], weight_ref[:, :half]) + nt(second_ref[0], weight_ref[:, half:])

    @pl.when(step == pl.num_programs(0) - 1)
    def _():
        inputs = inputs_ref[...].astype(WIDE)
        scale = rms_scale(inputs)
        grad = total[...]
        gain_grad_ref[...] = jnp.sum(grad * inputs * scale, axis=0, keepdims=True)
        scaled = gain_ref[...] * grad
        out_ref[...] = (
            hidden_grad_ref[...]
            + scale * scaled
            - inputs * (scale * scale * scale * jnp.mean(scaled * inputs, axis=-1, keepdims=True))
        ).astype(LOW)


def project_back_call(first, second, joint, grad_logits, extra, inputs, gain, hidden_grad, ready=()):
    parts, tokens, half = first.shape
    width = 2 * half

    def whole(shape):
        return pl.BlockSpec(shape, lambda j: (0,) * len(shape))

    return call_after(
        ready,
        project_back_kernel,
        grid=(parts,),
        in_specs=[
            pl.BlockSpec((1, tokens, half), lambda j: (j, 0, 0)),
            pl.BlockSpec((1, tokens, half), lambda j: (j, 0, 0)),
            pl.BlockSpec((width, width), lambda j: (0, j)),
            whole((tokens, 128)), whole((width, 128)),
            whole((tokens, width)), whole((1, width)), whole((tokens, width)),
        ],
        out_specs=[whole((tokens, width)), whole((1, width))],
        out_shape=[
            jax.ShapeDtypeStruct((tokens, width), LOW),
            jax.ShapeDtypeStruct((1, width), WIDE),
        ],
        scratch_shapes=[pltpu.VMEM((tokens, width), WIDE)],
        compiler_params=pltpu.CompilerParams(vmem_limit_bytes=VMEM_BYTES),
        cost_estimate=timed(10),
        name="project_back",
    )(first, second, joint, grad_logits, extra, inputs, gain, hidden_grad)


def back_kernel(
    first_head, cols_ref, rows_ref, beta_ref, taps_q, taps_k, taps_v, rim_q, rim_k, rim_v, in_q, in_k, in_v,
    solve_ref, weights_ref, state_ref, exit_ref, grad_ref,
    out_ref, edge_ref, tail_ref, tap_ref, rate_ref, room_ref, back_ref,
):
    cols, rows = cols_ref[0], rows_ref[0]
    row, column, inclusive, strict, tap_masks, carried, last = head_masks(cols, rows)
    beta_all = beta_ref[0]
    tap_count = taps_q.shape[0]
    size = cols.shape[0]
    heads = range(state_ref.shape[1])
    lanes = [slice(local * 128, (local + 1) * 128) for local in heads]
    parts = ((taps_q, rim_q, in_q), (taps_k, rim_k, in_k), (taps_v, rim_v, in_v))

    queries, keys, values, betas, kept = [], [], [], [], []
    for local in heads:
        acts = []
        for index, (taps, rim, block) in enumerate(parts):
            windows = windows_of(
                rim[0, :, lanes[local]].astype(WIDE),
                block[0, :, lanes[local]].astype(WIDE),
                tap_count,
                room_ref.at[3 * local + index],
            )
            convolved = convolve(windows, taps[:, lanes[local]].astype(WIDE), tap_masks)
            gate = jax.nn.sigmoid(convolved)
            acts.append(convolved * gate)
            kept.append(gate * (1.0 + convolved * (1.0 - gate)))
        queries.append(unit_and_scale(acts[0]))
        keys.append(unit_and_scale(acts[1]))
        values.append(acts[2])
        betas.append(pick_head(beta_all, first_head + local))
    eye = (row == column).astype(LOW)
    strict_low = jnp.where(strict, 1.0, 0.0).astype(LOW)
    inclusive_low = jnp.where(inclusive, 1.0, 0.0).astype(LOW)
    later_low = jnp.where(rows[0:1, :] == cols[:, 0:1], jnp.where(row <= column, 1.0, 0.0), 0.0).astype(LOW)
    later_strict_low = later_low - eye
    key_lows = [key.astype(LOW) for key, _ in keys]
    query_lows = [query.astype(LOW) for query, _ in queries]
    boths = [jnp.concatenate([key, query], axis=0) for key, query in zip(key_lows, query_lows)]
    grad_lows = [grad_ref[0, :, lanes[local]] for local in heads]
    scores_turned = [
        nt(key, query).astype(LOW) * later_low for key, query in zip(key_lows, query_lows)
    ]
    by_states = [nn(key_lows[i], state_ref[0, i]) for i in heads]
    freshes = [
        (weights_ref[0, i, :, 128:].astype(WIDE) - nn(weights_ref[0, i, :, :128], state_ref[0, i])).astype(LOW)
        for i in heads
    ]
    from_exit = [nn(key_lows[i], exit_ref[0, i]) for i in heads]
    solves_turned = [nt(eye, solve_ref[0, i]).astype(LOW) for i in heads]
    grad_fresh = [nn(scores_turned[i], grad_lows[i]) + last * from_exit[i] for i in heads]
    grad_right = [nn(solves_turned[i], grad_fresh[i]) for i in heads]
    sides = [
        jnp.concatenate([right.astype(LOW), grad], axis=0) for right, grad in zip(grad_right, grad_lows)
    ]
    outers = [nt(side, fresh).astype(LOW) for side, fresh in zip(sides, freshes)]
    outers_turned = [nt(fresh, side).astype(LOW) for side, fresh in zip(sides, freshes)]
    side_states = [nt(sides[i], state_ref[0, i]) for i in heads]
    grads = [
        jnp.concatenate([outer[:size] * strict_low, outer[size:] * inclusive_low], axis=0)
        for outer in outers
    ]
    grads_turned = [
        jnp.concatenate([outer[:, :size] * later_strict_low, outer[:, size:] * later_low], axis=1)
        for outer in outers_turned
    ]
    by_keys = [nn(grad, key) for grad, key in zip(grads, key_lows)]
    by_both = [
        nn(grads_turned[i], jnp.concatenate([(-betas[i] * keys[i][0]).astype(LOW), query_lows[i]], axis=0))
        for i in heads
    ]
    to_exit = [nt(freshes[i], exit_ref[0, i]) for i in heads]
    rates = [
        jnp.sum(
            grad_right[i] * (values[i] - carried * by_states[i]) - by_keys[i][:size] * keys[i][0],
            axis=1,
            keepdims=True,
        )
        for i in heads
    ]
    lane = lax.broadcasted_iota(jnp.int32, rate_ref.shape[1:], 1)
    rate_sum = jnp.zeros(rate_ref.shape[1:], WIDE)
    zeros = jnp.zeros((RIM, 128), WIDE)
    for local in heads:
        rate_sum = jnp.where(lane == first_head + local, rates[local], rate_sum)
        query, query_scale = queries[local]
        key, key_scale = keys[local]
        beta = betas[local]
        grad_query = carried * side_states[local][size:] + by_keys[local][size:]
        grad_key = (
            by_both[local]
            + last * to_exit[local]
            - beta * (by_keys[local][:size] + carried * side_states[local][:size])
        )
        grad_acts = (
            query_scale * (grad_query - query * jnp.sum(query * grad_query, axis=1, keepdims=True)),
            key_scale * (grad_key - key * jnp.sum(key * grad_key, axis=1, keepdims=True)),
            beta * grad_right[local],
        )
        for index in range(3):
            slot = 3 * local + index
            room = room_ref.at[slot]
            back = back_ref.at[slot]
            grad_conv = grad_acts[index] * kept[slot]
            weight = parts[index][0][:, lanes[local]].astype(WIDE)
            own = weight[0:1] * grad_conv
            edge_sum = zeros
            tap_ref[index, 0, 0:1, lanes[local]] = jnp.sum(
                grad_conv * room[pl.ds(RIM, size), :], axis=0, keepdims=True
            )
            for step in range(1, tap_count):
                masked = grad_conv * tap_masks[step - 1]
                tap_ref[index, 0, step : step + 1, lanes[local]] = jnp.sum(
                    masked * room[pl.ds(RIM - step, size), :], axis=0, keepdims=True
                )
                back[pl.ds(0, RIM), :] = zeros
                back[pl.ds(RIM, size), :] = weight[step : step + 1] * masked
                back[pl.ds(RIM + size, RIM), :] = zeros
                own = own + back[pl.ds(RIM + step, size), :]
                edge_sum = edge_sum + back[pl.ds(step, RIM), :]
            out_ref[index, 0, :, lanes[local]] = own.astype(LOW)
            edge_ref[index, 0, :, lanes[local]] = edge_sum
            tail_ref[index, 0, :, lanes[local]] = own[size - RIM :]
    rate_ref[0] = rate_sum * beta_all * (1.0 - beta_all)


def back_call(
    group, groups, cols, rows, beta, taps, rim, projected, solve, weights, state, exit_grad, grad, ready=()
):
    row_count, size, triple = projected.shape
    head_count = triple // (3 * 128)
    count = head_count // groups
    wide = count * 128
    tap_count = taps.shape[0]

    def of_row(block):
        return pl.BlockSpec(block, lambda r: (r, 0, 0))

    def part(rows_in, index):
        return pl.BlockSpec((1, rows_in, wide), lambda r: (r, 0, index * groups + group))

    def tap_part(index):
        return pl.BlockSpec((tap_count, wide), lambda r: (0, index * groups + group))

    def per_head(*block):
        return pl.BlockSpec((1, count) + block, lambda r: (r, group, 0, 0))

    def stacked(rows_in):
        return pl.BlockSpec((3, 1, rows_in, wide), lambda r: (0, r, 0, 0))

    def stacked_type(rows_in, kind):
        return jax.ShapeDtypeStruct((3, row_count, rows_in, wide), kind)

    return call_after(
        ready,
        functools.partial(back_kernel, group * count),
        grid=(row_count,),
        in_specs=[of_row((1,) + cols.shape[1:]), of_row((1,) + rows.shape[1:]), of_row((1,) + beta.shape[1:])]
        + [tap_part(i) for i in range(3)]
        + [part(RIM, i) for i in range(3)]
        + [part(size, i) for i in range(3)]
        + [per_head(size, size), per_head(size, 256), per_head(128, 128), per_head(128, 128), part(size, 0)],
        out_specs=[
            stacked(size), stacked(RIM), stacked(RIM), stacked(tap_count), of_row((1, size, 128)),
        ],
        out_shape=[
            stacked_type(size, LOW), stacked_type(RIM, WIDE), stacked_type(RIM, WIDE),
            stacked_type(tap_count, WIDE),
            jax.ShapeDtypeStruct((row_count, size, 128), WIDE),
        ],
        scratch_shapes=[
            pltpu.VMEM((3 * count, RIM + size, 128), WIDE),
            pltpu.VMEM((3 * count, size + 2 * RIM, 128), WIDE),
        ],
        compiler_params=pltpu.CompilerParams(vmem_limit_bytes=VMEM_BYTES),
        cost_estimate=timed(36 / groups),
        name="mixer_back",
    )(
        cols, rows, beta, taps, taps, taps, rim, rim, rim, projected, projected, projected,
        solve, weights, state, exit_grad, grad,
    )


def timed(microseconds):
    return pl.CostEstimate(
        flops=int(microseconds * 1.0e9), bytes_accessed=int(microseconds * 1.0e6), transcendentals=0
    )


def shifted(value, axis, steps):
    count = lax.axis_size(axis)
    leading, last = (max(0, -steps), min(count, count - steps))
    return lax.ppermute(value, axis, [(source, source + steps) for source in range(leading, last)])


def swap(value, bit):
    count = lax.axis_size("seq")
    return lax.ppermute(value, "seq", [(source, source ^ bit) for source in range(count)])


def put(outs, pieces, moves, position):
    for piece, parts in zip(pieces, moves):
        for member, relative, rows, start, source, count in parts:
            target = pl.multiple_of((position ^ relative) * rows + start, 16)
            outs[member][pl.ds(target, count), :] = piece[source : source + count, :]


def place_kernel(moves, position_ref, *refs):
    put(refs[len(moves) :], refs[: len(moves)], moves, position_ref[0])


def place(gathered):
    pieces, moves, sizes, position = gathered
    columns = pieces[0].shape[1]
    tile = next(size for size in (1408, 1024, 512, 256, 128) if columns % size == 0)
    return pl.pallas_call(
        functools.partial(place_kernel, moves),
        grid=(columns // tile,),
        in_specs=[pl.BlockSpec(memory_space=pltpu.SMEM)]
        + [pl.BlockSpec((piece.shape[0], tile), lambda j: (0, j)) for piece in pieces],
        out_specs=[pl.BlockSpec((size, tile), lambda j: (0, j)) for size in sizes],
        out_shape=[jax.ShapeDtypeStruct((size, columns), pieces[0].dtype) for size in sizes],
        compiler_params=pltpu.CompilerParams(vmem_limit_bytes=VMEM_BYTES),
        cost_estimate=timed(1 + sum(sizes) * columns / 1.2e6),
        name="place",
    )(position, *pieces)


def join(*values):
    return lax.optimization_barrier(values)


def gather_near(shard):
    return (swap(shard, 2), swap(shard, 4)) if seq_is_cube() else None


def gather_far(near):
    if not seq_is_cube():
        return None
    by_x, by_y = near
    half = by_x.shape[0] // 2
    return swap(by_x[:half], 4), swap(by_y[half:], 2)


def gather_core(shard, near, far):
    if not seq_is_cube():
        return [lax.all_gather(shard, "seq", axis=0)]
    mine = jnp.concatenate([shard, *near, *far], axis=0)
    return [mine, swap(mine, 1)]


def gather_core_parts(shard, near, far):
    if not seq_is_cube():
        return [lax.all_gather(shard, "seq", axis=0)]
    mine = [shard, *near, *far]
    return mine + [swap(piece, 1) for piece in mine]


def placing(pieces, sizes):
    count = lax.axis_size("seq")
    if not seq_is_cube():
        parts, moves, offset = [], [], 0
        for member, size in enumerate(sizes):
            parts.append(pieces[0][:, offset : offset + size].reshape(count * size, -1))
            moves.append(((member, 0, 0, 0, 0, count * size),))
            offset += size
        return parts, tuple(moves), tuple(count * size for size in sizes), jnp.zeros((1,), jnp.int32)
    rows = sum(sizes)
    half = rows // 2
    spans = [(0, 0, rows), (2, 0, rows), (4, 0, rows), (6, 0, half), (6, half, half)]
    spans += [(relative ^ 1, first, span) for relative, first, span in spans]
    moves, index, source = [], 0, 0
    parts = []
    for relative, first, span in spans:
        offset = 0
        for member, size in enumerate(sizes):
            low, high = max(first, offset), min(first + span, offset + size)
            if low < high:
                parts.append((member, relative, size, low - offset, source + low - first, high - low))
            offset += size
        source += span
        if source == pieces[index].shape[0]:
            moves.append(tuple(parts))
            parts, index, source = [], index + 1, 0
    position = lax.axis_index("seq").astype(jnp.int32).reshape(1)
    return pieces, tuple(moves), tuple(count * size for size in sizes), position


def project_kernel(
    moves, piece_count, position_ref, inputs_ref, valid_ref, bias_ref, *refs
):
    pieces, extra_pieces = refs[:piece_count], refs[piece_count : 2 * piece_count]
    joint_ref, extra_ref, normed_ref, out_ref, beta_ref, extras_ref = refs[2 * piece_count :]
    put([joint_ref], pieces, moves, position_ref[0])

    @pl.when(pl.program_id(0) == 0)
    def _():
        put([extra_ref], extra_pieces, moves, position_ref[0])
        extra = extra_ref[...]
        row = lax.broadcasted_iota(jnp.int32, (16, 128), 0)
        lane = lax.broadcasted_iota(jnp.int32, (16, 128), 1)
        extras = nt(jnp.where(lane == row + 8, 1.0, 0.0), extra)
        extras_ref[...] = extras
        inputs = inputs_ref[...].astype(WIDE)
        normed = (inputs * rms_scale(inputs) * extras[0:1]).astype(LOW)
        normed_ref[...] = normed
        beta_ref[...] = valid_ref[:, 0:1] * jax.nn.sigmoid(nn(normed, extra) + bias_ref[...])

    out_ref[...] = nn(normed_ref[...], joint_ref[...]).astype(LOW)


def project_call(gathered, inputs, valid, bias):
    pieces, moves, sizes, position = gathered
    tokens, width = inputs.shape
    columns = pieces[0].shape[1] - 128
    tile = 1024

    def whole(shape):
        return pl.BlockSpec(shape, lambda j: (0,) * len(shape))

    last = columns // 128
    return pl.pallas_call(
        functools.partial(project_kernel, moves, len(pieces)),
        grid=(columns // tile,),
        in_specs=[
            pl.BlockSpec(memory_space=pltpu.SMEM), whole((tokens, width)), whole(valid.shape), whole(bias.shape),
        ]
        + [pl.BlockSpec((piece.shape[0], tile), lambda j: (0, j)) for piece in pieces]
        + [pl.BlockSpec((piece.shape[0], 128), lambda j: (0, last)) for piece in pieces],
        out_specs=[
            pl.BlockSpec((width, tile), lambda j: (0, j)), whole((width, 128)), whole((tokens, width)),
            pl.BlockSpec((tokens, tile), lambda j: (0, j)), whole((tokens, 128)), whole((16, width)),
        ],
        out_shape=[
            jax.ShapeDtypeStruct((width, columns), LOW),
            jax.ShapeDtypeStruct((width, 128), LOW),
            jax.ShapeDtypeStruct((tokens, width), LOW),
            jax.ShapeDtypeStruct((tokens, columns), LOW),
            jax.ShapeDtypeStruct((tokens, 128), WIDE),
            jax.ShapeDtypeStruct((16, width), WIDE),
        ],
        compiler_params=pltpu.CompilerParams(vmem_limit_bytes=VMEM_BYTES),
        cost_estimate=timed(10),
        name="project",
    )(position, inputs, valid, bias, *pieces, *pieces)


def join(*values):
    return lax.optimization_barrier(values)


def gather_near(shard):
    return (swap(shard, 2), swap(shard, 4)) if seq_is_cube() else None


def gather_far(near):
    if not seq_is_cube():
        return None
    by_x, by_y = near
    half = by_x.shape[0] // 2
    return swap(by_x[:half], 4), swap(by_y[half:], 2)


def gather_core(shard, near, far):
    if not seq_is_cube():
        return [lax.all_gather(shard, "seq", axis=0)]
    mine = [shard, *near, *far]
    return mine + [swap(piece, 1) for piece in mine]


def placing(pieces, sizes):
    count = lax.axis_size("seq")
    if not seq_is_cube():
        parts, moves, offset = [], [], 0
        for member, size in enumerate(sizes):
            parts.append(pieces[0][:, offset : offset + size].reshape(count * size, -1))
            moves.append(((member, 0, 0, 0, 0, count * size),))
            offset += size
        return parts, tuple(moves), tuple(count * size for size in sizes), jnp.zeros((1,), jnp.int32)
    rows = sum(sizes)
    half = rows // 2
    spans = [(0, 0, rows), (2, 0, rows), (4, 0, rows), (6, 0, half), (6, half, half)]
    spans += [(relative ^ 1, first, span) for relative, first, span in spans]
    moves = []
    for relative, first, span in spans:
        parts, offset = [], 0
        for member, size in enumerate(sizes):
            low, high = max(first, offset), min(first + span, offset + size)
            if low < high:
                parts.append((member, relative, size, low - offset, low - first, high - low))
            offset += size
        moves.append(tuple(parts))
    position = lax.axis_index("seq").astype(jnp.int32).reshape(1)
    return pieces, tuple(moves), tuple(count * size for size in sizes), position


def project_kernel(
    moves, piece_count, position_ref, inputs_ref, valid_ref, bias_ref, *refs
):
    pieces, extra_pieces = refs[:piece_count], refs[piece_count : 2 * piece_count]
    joint_ref, extra_ref, normed_ref, out_ref, beta_ref, extras_ref = refs[2 * piece_count :]
    put([joint_ref], pieces, moves, position_ref[0])

    @pl.when(pl.program_id(0) == 0)
    def _():
        put([extra_ref], extra_pieces, moves, position_ref[0])
        extra = extra_ref[...]
        row = lax.broadcasted_iota(jnp.int32, (16, 128), 0)
        lane = lax.broadcasted_iota(jnp.int32, (16, 128), 1)
        extras = nt(jnp.where(lane == row + 8, 1.0, 0.0), extra)
        extras_ref[...] = extras
        inputs = inputs_ref[...].astype(WIDE)
        normed = (inputs * rms_scale(inputs) * extras[0:1]).astype(LOW)
        normed_ref[...] = normed
        beta_ref[...] = valid_ref[:, 0:1] * jax.nn.sigmoid(nn(normed, extra) + bias_ref[...])

    out_ref[...] = nn(normed_ref[...], joint_ref[...]).astype(LOW)


def project_call(gathered, inputs, valid, bias):
    pieces, moves, sizes, position = gathered
    tokens, width = inputs.shape
    columns = pieces[0].shape[1] - 128
    tile = 1024

    def whole(shape):
        return pl.BlockSpec(shape, lambda j: (0,) * len(shape))

    last = columns // 128
    return pl.pallas_call(
        functools.partial(project_kernel, moves, len(pieces)),
        grid=(columns // tile,),
        in_specs=[
            pl.BlockSpec(memory_space=pltpu.SMEM), whole((tokens, width)), whole(valid.shape), whole(bias.shape),
        ]
        + [pl.BlockSpec((piece.shape[0], tile), lambda j: (0, j)) for piece in pieces]
        + [pl.BlockSpec((piece.shape[0], 128), lambda j: (0, last)) for piece in pieces],
        out_specs=[
            pl.BlockSpec((width, tile), lambda j: (0, j)), whole((width, 128)), whole((tokens, width)),
            pl.BlockSpec((tokens, tile), lambda j: (0, j)), whole((tokens, 128)), whole((16, width)),
        ],
        out_shape=[
            jax.ShapeDtypeStruct((width, columns), LOW),
            jax.ShapeDtypeStruct((width, 128), LOW),
            jax.ShapeDtypeStruct((tokens, width), LOW),
            jax.ShapeDtypeStruct((tokens, columns), LOW),
            jax.ShapeDtypeStruct((tokens, 128), WIDE),
            jax.ShapeDtypeStruct((16, width), WIDE),
        ],
        compiler_params=pltpu.CompilerParams(vmem_limit_bytes=VMEM_BYTES),
        cost_estimate=timed(10),
        name="project",
    )(position, inputs, valid, bias, *pieces, *pieces)


def after(value, *earlier):
    return lax.optimization_barrier((value, earlier))[0]


def outer_turn_kernel(order_ref, left_ref, right_ref, out_ref, other_ref, own_ref, turned):
    rows = out_ref.shape[1]

    @pl.when(pl.program_id(0) == 0)
    def _():
        turned[...] = left_ref[...].T
        for index in range(4):
            first = pl.multiple_of(order_ref[index] * rows, 16)
            other_ref[index * rows : (index + 1) * rows, :] = turned[pl.ds(first, rows), :]
            second = pl.multiple_of(order_ref[4 + index] * rows, 16)
            own_ref[index * rows : (index + 1) * rows, :] = turned[pl.ds(second, rows), :]

    out_ref[...] = nn(other_ref[...], right_ref[0]).astype(LOW).reshape(out_ref.shape)


def outer_kernel(left_ref, right_ref, out_ref):
    out_ref[...] = nn(left_ref[...], right_ref[0]).astype(LOW).reshape(out_ref.shape)


def outer_add_kernel(left_ref, right_ref, add_ref, out_ref):
    total = nn(left_ref[...], right_ref[0])
    out_ref[...] = (
        (total + add_ref[...].reshape(total.shape).astype(WIDE)).astype(LOW).reshape(out_ref.shape)
    )


def outer_tile(parts, columns):
    sizes = (2816, 1024, 512, 256) if parts > 1 else (512, 256)
    return next(size for size in sizes if columns % size == 0)


def outer_specs(left_rows, right):
    parts, tokens, columns = right.shape
    rows = left_rows // 4
    tile = outer_tile(parts, columns)
    steps = columns // tile
    return dict(
        grid=(parts * steps,),
        left=pl.BlockSpec((left_rows, tokens), lambda j: (0, 0)),
        right=pl.BlockSpec((1, tokens, tile), lambda j: (j // steps, 0, j % steps)),
        out=pl.BlockSpec((4, rows, tile), lambda j: (0, 0, j)),
        out_type=jax.ShapeDtypeStruct((4, rows, parts * columns), LOW),
        params=pltpu.CompilerParams(vmem_limit_bytes=VMEM_BYTES),
        cost=timed(1 + tokens * left_rows * parts * columns / 1.8e8),
    )


def seq_is_cube():
    return lax.axis_size("seq") == 8


def outer_turn(left, right, position, ready=()):
    tokens, features = left.shape
    if not seq_is_cube():
        return None, left, left
    specs = outer_specs(features // 2, right)
    order = position ^ jnp.array([1, 3, 5, 7, 0, 2, 4, 6], jnp.int32)
    left_type = jax.ShapeDtypeStruct((features // 2, tokens), LOW)
    return call_after(
        ready,
        outer_turn_kernel,
        grid=specs["grid"],
        in_specs=[
            pl.BlockSpec(memory_space=pltpu.SMEM),
            pl.BlockSpec((tokens, features), lambda j: (0, 0)),
            specs["right"],
        ],
        out_specs=[specs["out"], specs["left"], specs["left"]],
        out_shape=[specs["out_type"], left_type, left_type],
        scratch_shapes=[pltpu.VMEM((features, tokens), LOW)],
        compiler_params=specs["params"],
        cost_estimate=specs["cost"],
        name="outer_turn",
    )(order, left, right)


def outer(left, right, ready=()):
    if not seq_is_cube():
        return None
    specs = outer_specs(left.shape[0], right)
    return call_after(
        ready,
        outer_kernel,
        grid=specs["grid"],
        in_specs=[specs["left"], specs["right"]],
        out_specs=specs["out"],
        out_shape=specs["out_type"],
        compiler_params=specs["params"],
        cost_estimate=specs["cost"],
        name="outer",
    )(left, right)


def outer_add(left, right, received, ready=()):
    if not seq_is_cube():
        full = [jnp.einsum("td,te->de", left, right[i], preferred_element_type=WIDE) for i in range(right.shape[0])]
        full = jnp.concatenate(full, axis=-1).astype(LOW)
        return lax.psum_scatter(full, "seq", scatter_dimension=0, tiled=True)
    specs = outer_specs(left.shape[0], right)
    return call_after(
        ready,
        outer_add_kernel,
        grid=specs["grid"],
        in_specs=[specs["left"], specs["right"], specs["out"]],
        out_specs=specs["out"],
        out_shape=specs["out_type"],
        compiler_params=specs["params"],
        cost_estimate=specs["cost"],
        name="outer_add",
    )(left, right, received)


def outer_two_turn_kernel(
    order_ref, left_a, left_b, right_a, right_b, out_ref, own_a, own_b, turned_a, turned_b, other_a, other_b
):
    first_rows = other_a.shape[0] // 4

    @pl.when(pl.program_id(0) == 0)
    def _():
        for left, turned, other, own in ((left_a, turned_a, other_a, own_a), (left_b, turned_b, other_b, own_b)):
            rows = other.shape[0] // 4
            turned[...] = left[...].T
            for index in range(4):
                first = pl.multiple_of(order_ref[index] * rows, 16)
                other[index * rows : (index + 1) * rows, :] = turned[pl.ds(first, rows), :]
                second = pl.multiple_of(order_ref[4 + index] * rows, 16)
                own[index * rows : (index + 1) * rows, :] = turned[pl.ds(second, rows), :]

    tile = out_ref.shape[2]
    out_ref[:, :first_rows] = nn(other_a[...], right_a[...]).astype(LOW).reshape(4, -1, tile)
    out_ref[:, first_rows:] = nn(other_b[...], right_b[...]).astype(LOW).reshape(4, -1, tile)


def outer_two_add_kernel(left_a, left_b, right_a, right_b, add_ref, out_ref):
    first_rows = left_a.shape[0] // 4
    tile = out_ref.shape[2]
    for left, right, rows in (
        (left_a, right_a, slice(0, first_rows)), (left_b, right_b, slice(first_rows, out_ref.shape[1]))
    ):
        total = nn(left[...], right[...]).reshape(4, -1, tile)
        out_ref[:, rows] = (total + add_ref[:, rows].astype(WIDE)).astype(LOW)


def outer_two_turn(lefts, rights, position, ready=()):
    if not seq_is_cube():
        return None, lefts
    tokens, columns = rights[0].shape
    halves = [left.shape[1] // 2 for left in lefts]
    rows = sum(halves) // 4
    tile = 512
    order = position ^ jnp.array([1, 3, 5, 7, 0, 2, 4, 6], jnp.int32)
    whole = [pl.BlockSpec(left.shape, lambda j: (0, 0)) for left in lefts]
    half_specs = [pl.BlockSpec((half, tokens), lambda j: (0, 0)) for half in halves]
    right_spec = pl.BlockSpec((tokens, tile), lambda j: (0, j))
    other, *own = call_after(
        ready,
        outer_two_turn_kernel,
        grid=(columns // tile,),
        in_specs=[pl.BlockSpec(memory_space=pltpu.SMEM), *whole, right_spec, right_spec],
        out_specs=[pl.BlockSpec((4, rows, tile), lambda j: (0, 0, j)), *half_specs],
        out_shape=[
            jax.ShapeDtypeStruct((4, rows, columns), LOW),
            *[jax.ShapeDtypeStruct((half, tokens), LOW) for half in halves],
        ],
        scratch_shapes=[pltpu.VMEM((2 * half, tokens), LOW) for half in halves]
        + [pltpu.VMEM((half, tokens), LOW) for half in halves],
        compiler_params=pltpu.CompilerParams(vmem_limit_bytes=VMEM_BYTES),
        cost_estimate=timed(12),
        name="outer_two_turn",
    )(order, *lefts, *rights)
    return other, own


def outer_two_add(lefts, rights, received, ready=()):
    if not seq_is_cube():
        return jnp.concatenate(
            [outer_add(left, right[None], None) for left, right in zip(lefts, rights)], axis=0
        )
    tokens, columns = rights[0].shape
    rows = sum(left.shape[0] for left in lefts) // 4
    tile = 512
    right_spec = pl.BlockSpec((tokens, tile), lambda j: (0, j))
    out_spec = pl.BlockSpec((4, rows, tile), lambda j: (0, 0, j))
    return call_after(
        ready,
        outer_two_add_kernel,
        grid=(columns // tile,),
        in_specs=[pl.BlockSpec(left.shape, lambda j: (0, 0)) for left in lefts] + [right_spec, right_spec, out_spec],
        out_specs=out_spec,
        out_shape=jax.ShapeDtypeStruct((4, rows, columns), LOW),
        compiler_params=pltpu.CompilerParams(vmem_limit_bytes=VMEM_BYTES),
        cost_estimate=timed(9),
        name="outer_two_add",
    )(*lefts, *rights, received)


def send_other(other):
    return swap(other, 1) if seq_is_cube() else None


def scatter_far(own):
    if not seq_is_cube():
        return own
    half = own.shape[1] // 2
    return own, swap(own[3, :half], 2), swap(own[3, half:], 4)


def scatter_mid(stage):
    if not seq_is_cube():
        return stage
    own, to_second, to_first = stage
    half = own.shape[1] // 2
    first = jnp.concatenate(
        [own[1, :half], (own[1, half:].astype(WIDE) + to_first.astype(WIDE)).astype(LOW)], axis=0
    )
    second = jnp.concatenate(
        [(own[2, :half].astype(WIDE) + to_second.astype(WIDE)).astype(LOW), own[2, half:]], axis=0
    )
    return own[0], first, second


def scatter_near(stage):
    if not seq_is_cube():
        return stage
    own, first, second = stage
    return own, swap(first, 2), swap(second, 4)


def scatter_end(stage):
    if not seq_is_cube():
        return stage
    own, by_x, by_y = stage
    return (own.astype(WIDE) + by_x.astype(WIDE) + by_y.astype(WIDE)).astype(LOW)


def rows_are_line():
    return lax.axis_size("row") == 4


def row_inward(value):
    if not rows_are_line():
        return lax.psum(value, "row")
    return value, lax.ppermute(value, "row", [(0, 1), (3, 2)])


def row_across(stage):
    if not rows_are_line():
        return stage
    value, received = stage
    value = (value.astype(WIDE) + received.astype(WIDE)).astype(value.dtype)
    return value, lax.ppermute(value, "row", [(1, 2), (2, 1)])


def row_outward(stage):
    if not rows_are_line():
        return stage
    value, received = stage
    value = (value.astype(WIDE) + received.astype(WIDE)).astype(value.dtype)
    return value, lax.ppermute(value, "row", [(1, 0), (2, 3)])


def row_end(stage):
    if not rows_are_line():
        return stage.astype(WIDE)
    value, received = stage
    index = lax.axis_index("row")
    return jnp.where((index == 0) | (index == 3), received, value).astype(WIDE)


def on_device(
    inputs,
    lengths,
    norm_gain,
    w_qkv,
    w_beta,
    beta_bias,
    w_conv,
    w_out,
    ffn_gain,
    w_gate,
    w_up,
    w_down,
    cotangent,
):
    row_count, slot_count, width = inputs.shape
    token_count = row_count * slot_count
    head_count = beta_bias.shape[0]
    tap_count = w_conv.shape[0]
    rim_size = tap_count - 1
    pairs = row_count * head_count
    shard = norm_gain.shape[0]
    seq_count = lax.axis_size("seq")
    position = lax.axis_index("seq").astype(jnp.int32)

    by_lane = jnp.transpose(w_conv.reshape(tap_count, 3, shard), (2, 0, 1)).reshape(shard, -1)
    extra = jnp.concatenate([w_beta, norm_gain[:, None], ffn_gain[:, None], by_lane], axis=1)
    extra = jnp.pad(extra, ((0, 0), (0, 128 - extra.shape[1])))
    w_joint = jnp.concatenate([w_qkv, extra], axis=1)
    joint_near = gather_near(w_joint)
    doc_ends = jnp.cumsum(lengths, axis=1, dtype=jnp.int32)
    spots = position * slot_count - rim_size + jnp.arange(slot_count + rim_size, dtype=jnp.int32)
    ext_docs = jnp.sum(
        (spots[None, :, None] >= doc_ends[:, None, :]).astype(jnp.int32), axis=2, dtype=jnp.int32
    )
    ext_docs = jnp.where(spots[None, :] < 0, -1, ext_docs)
    own_docs = ext_docs[:, rim_size:]
    valid_mask = (spots[None, rim_size:] < doc_ends[:, -1:]).astype(WIDE)
    shown = [own_docs.astype(WIDE)]
    for offset in range(1, tap_count):
        before = ext_docs[:, rim_size - offset : rim_size - offset + slot_count]
        shown.append((before == own_docs).astype(WIDE))
    shown.append((own_docs == ext_docs[:, rim_size - 1 : rim_size]).astype(WIDE))
    shown.append((own_docs == own_docs[:, -1:]).astype(WIDE))
    shown += [valid_mask, valid_mask]
    cols = jnp.stack(shown, axis=-1)
    valid = jnp.broadcast_to(valid_mask.reshape(token_count, 1), (token_count, 8))
    rows = jnp.broadcast_to(own_docs.astype(WIDE)[:, None, :], (row_count, 8, slot_count))
    bounds = jnp.arange(seq_count, dtype=jnp.int32) * slot_count
    doc_first = jnp.sum((bounds[None, :, None] - 1 >= doc_ends[:, None, :]).astype(jnp.int32), axis=2)
    doc_last = jnp.sum(
        (bounds[None, :, None] + slot_count - 1 >= doc_ends[:, None, :]).astype(jnp.int32), axis=2
    )
    keep = (doc_first == doc_last).astype(WIDE)
    share = -(-pairs // seq_count)
    keep_pairs = jnp.pad(
        jnp.repeat(keep, head_count, axis=0), ((0, share * seq_count - pairs), (0, 0))
    )
    keep_own = lax.dynamic_slice_in_dim(keep_pairs, position * share, share, axis=0)

    joint_near, cols, rows, valid, keep_own = join(joint_near, cols, rows, valid, keep_own)
    joint_far = gather_far(joint_near)
    joint_far, gate_shard = join(joint_far, w_gate)
    joint_pieces = placing(gather_core_parts(w_joint, joint_near, joint_far), (shard,))
    gate_near = gather_near(gate_shard)

    tokens_in = inputs.reshape(token_count, width)
    bias_row = jnp.pad(beta_bias.astype(WIDE), (0, 128 - head_count))[None]
    joint, joint_extra, normed, projected, beta, extras = project_call(
        joint_pieces, tokens_in, valid, bias_row
    )
    first_gain, second_gain = extras[0:1], extras[1:2]
    taps = extras[2 : 2 + 3 * tap_count].reshape(tap_count, 3, seq_count, shard)
    taps = jnp.swapaxes(taps, 1, 2).reshape(tap_count, 3 * width).astype(LOW)
    projected = projected.reshape(row_count, slot_count, 3 * width)
    beta = beta.reshape(row_count, slot_count, 128)
    rim = shifted(projected[:, slot_count - RIM :], "seq", 1)

    rim, projected, gate_near, up_shard = join(rim, projected, gate_near, w_up)
    gate_far = gather_far(gate_near)
    up_near = gather_near(up_shard)
    w_rest = jnp.concatenate([w_out, w_down], axis=0)
    eff, local_out, maps, solve, weights = prepare_call(cols, rows, beta, taps, rim, projected)
    maps, gate_far, up_near, w_rest = join(maps, gate_far, up_near, w_rest)
    up_far = gather_far(up_near)
    maps_here = exchange(maps.reshape((pairs,) + maps.shape[2:]), seq_count)
    gate_pieces = placing(gather_core(gate_shard, gate_near, gate_far), (shard,))
    maps_here, up_far, gate_whole, rest_shard = join(maps_here, up_far, gate_pieces[0], w_rest)
    gate_pieces = (gate_whole,) + gate_pieces[1:]
    states_here = chain_call(chain_forward_kernel, keep_own, maps_here)
    rest_near = gather_near(rest_shard)
    state = to_home(states_here, pairs).reshape((row_count, head_count, 128, 128))
    up_pieces = placing(gather_core(up_shard, up_near, up_far), (shard,))
    state, rest_near = join(state, rest_near)
    rest_far = gather_far(rest_near)
    full_out, full_down = place(
        placing(gather_core_parts(w_rest, rest_near, rest_far), (shard, w_down.shape[0]))
    )

    (
        heads_low, second, act, grad_pair, output, upstream_low,
        grad_hidden, grad_mix_low, grad_heads, local_grad, grad_ffn_gain,
    ) = feed_call(
        eff, local_out, state, tokens_in, cotangent.reshape(token_count, width), valid, second_gain,
        full_out, gate_pieces, up_pieces, full_down,
    )
    grad_heads = grad_heads.reshape(row_count, slot_count, width)

    grads_here = exchange(local_grad.reshape((pairs, 128, 128)), seq_count)
    other_pair, _, left_pair = outer_turn(second, grad_pair, position)
    from_pair = send_other(other_pair)
    exits_here = chain_call(chain_backward_kernel, keep_own, maps_here, grads_here, ready=left_pair)
    exit_grad = to_home(exits_here, pairs).reshape((row_count, head_count, 128, 128))
    rights = (grad_mix_low, upstream_low)
    other_rest, left_rest = outer_two_turn((heads_low, act), rights, position, ready=exits_here)
    from_rest = send_other(other_rest)
    own_pair = outer_add(left_pair, grad_pair, from_pair, ready=left_rest)
    exit_grad, own_pair = join(exit_grad, own_pair)
    far_pair = scatter_far(own_pair)

    def pull(group, ready):
        grad_parts, edges, tails, tap_sums, logits = back_call(
            group, 2, cols, rows, beta, taps, rim, projected, solve, weights, state, exit_grad, grad_heads, ready
        )
        return grad_parts, shifted(edges.astype(LOW), "seq", -1), tails, jnp.sum(tap_sums, axis=1), logits

    def fix(grad_parts, back_rim, tails):
        fixed = lax.dynamic_update_slice(
            grad_parts, (tails + back_rim.astype(WIDE)).astype(LOW), (0, 0, slot_count - RIM, 0)
        )
        return fixed.reshape(3, token_count, -1)

    first_parts, first_rim, first_tails, first_taps, first_logits = pull(0, own_pair)
    far_pair, first_logits, from_rest = join(far_pair, first_logits, from_rest)
    own_rest = outer_two_add(left_rest, rights, from_rest, ready=first_logits)
    first_rim, own_rest, first_parts, far_pair = join(first_rim, own_rest, first_parts, far_pair)
    mid_pair = scatter_mid(far_pair)
    near_pair = scatter_near(mid_pair)
    first_grad = fix(first_parts, first_rim, first_tails)
    other_first, left_other, left_own = outer_turn(normed, first_grad, position, ready=mid_pair)
    from_first = send_other(other_first)
    second_parts, second_rim, second_tails, second_taps, second_logits = pull(1, (left_own, mid_pair))
    near_pair, from_first, second_logits, own_rest = join(near_pair, from_first, second_logits, own_rest)
    pair = scatter_end(near_pair)
    units = w_gate.shape[1]
    gate, up = row_inward(pair[:, :units]), row_inward(pair[:, units:])
    far_rest = scatter_far(own_rest)
    own_first = outer_add(left_own, first_grad, from_first, ready=(second_logits, gate[0], up[0]))
    second_rim, second_parts, own_first, far_rest = join(second_rim, second_parts, own_first, far_rest)
    far_first = scatter_far(own_first)
    bias = jnp.sum(first_logits + second_logits, axis=(0, 1))[None]
    if seq_is_cube():
        bias = bias + swap(bias, 1)
        bias = bias + swap(bias, 2)
    mid_rest = scatter_mid(far_rest)
    second_grad = fix(second_parts, second_rim, second_tails)
    other_second = outer(left_other, second_grad, ready=mid_rest)
    far_first, other_second, gate, up, bias, mid_rest = join(
        far_first, other_second, gate, up, bias, mid_rest
    )
    from_second = send_other(other_second)
    gate, up = row_across(gate), row_across(up)
    near_rest = scatter_near(mid_rest)
    mid_first = scatter_mid(far_first)

    grad_logits = (first_logits + second_logits).reshape(token_count, 128)
    grad_inputs, grad_norm_gain = project_back_call(
        first_grad, second_grad, joint, grad_logits, joint_extra, tokens_in, first_gain, grad_hidden,
        ready=(other_second, mid_first, gate[0], up[0]),
    )
    grad_beta_w = jnp.einsum(
        "td,th->dh", normed.astype(WIDE), grad_logits[:, :head_count], precision=lax.Precision.HIGHEST
    )
    grad_conv_w = jnp.stack([first_taps, second_taps], axis=2)
    grad_conv_w = jnp.swapaxes(grad_conv_w, 0, 1).reshape(tap_count, seq_count, 3, shard)
    minor = jnp.concatenate(
        [
            grad_beta_w.reshape(seq_count, shard, head_count),
            grad_norm_gain.reshape(seq_count, shard, 1),
            grad_ffn_gain.reshape(seq_count, shard, 1),
            jnp.transpose(grad_conv_w, (1, 3, 0, 2)).reshape(seq_count, shard, 3 * tap_count),
        ],
        axis=2,
    )
    minor = jnp.pad(minor, ((0, 0), (0, 0), (0, 128 - minor.shape[2])))
    if seq_is_cube():
        order = position ^ jnp.array([1, 3, 5, 7, 0, 2, 4, 6], jnp.int32)
        minor = jnp.take(minor, order, axis=0)
        own_minor = (minor[4:] + swap(minor[:4].astype(LOW), 1).astype(WIDE)).astype(LOW)
    else:
        own_minor = lax.psum_scatter(
            minor.reshape(width, 128).astype(LOW), "seq", scatter_dimension=0, tiled=True
        )
    from_second, grad_inputs, own_minor, near_rest, gate = join(
        from_second, grad_inputs, own_minor, near_rest, gate
    )
    gate = row_outward(gate)
    rest = row_inward(scatter_end(near_rest))
    near_first = scatter_near(mid_first)
    own_second = jnp.concatenate(
        [outer_add(left_own, second_grad, from_second, ready=(gate[0], rest[0])), own_minor], axis=-1
    )
    own_second, near_first = join(own_second, near_first)
    far_second = scatter_far(own_second)
    shard_first = scatter_end(near_first)
    far_second, rest, up, gate, shard_first, bias = join(far_second, rest, up, gate, shard_first, bias)
    near_second = scatter_near(scatter_mid(far_second))
    rest = row_across(rest)
    up = row_outward(up)
    first = row_inward(shard_first)
    if seq_is_cube():
        bias = bias + swap(bias, 4)
    total_gate = row_end(gate)
    near_second, rest, up, bias, first, total_gate = join(near_second, rest, up, bias, first, total_gate)
    second_ = row_inward(scatter_end(near_second))
    first = row_across(first)
    rest = row_outward(rest)
    bias = row_inward(bias) if seq_is_cube() else bias
    total_up = row_end(up)
    second_, rest, first, bias, total_up = join(second_, rest, first, bias, total_up)
    second_ = row_across(second_)
    first = row_outward(first)
    bias = row_across(bias) if seq_is_cube() else bias
    total_rest = row_end(rest)
    first, second_, bias, total_rest = join(first, second_, bias, total_rest)
    second_ = row_outward(second_)
    bias = row_end(row_outward(bias)) if seq_is_cube() else lax.psum(bias, ("seq", "row"))
    total_first = row_end(first)
    second_, bias, total_first = join(second_, bias, total_first)
    total_second = row_end(second_)
    bias_total = bias[0, :head_count]
    total_out, total_down = total_rest[:shard], total_rest[shard:]
    half = width // 2
    total_qkv = jnp.concatenate(
        [
            total[:, part * half : (part + 1) * half]
            for part in range(3)
            for total in (total_first, total_second)
        ],
        axis=1,
    )
    small = total_second[:, 3 * half :]
    columns = head_count + 2
    total_conv = jnp.transpose(
        small[:, columns : columns + 3 * tap_count].reshape(shard, tap_count, 3), (1, 2, 0)
    ).reshape(tap_count, -1)
    return (
        output.reshape(inputs.shape),
        grad_inputs.reshape(inputs.shape),
        small[:, head_count],
        total_qkv,
        small[:, :head_count],
        bias_total,
        total_conv,
        total_out,
        small[:, head_count + 1],
        total_gate,
        total_up,
        total_down,
    )


def solution(mesh):
    placed = (
        P("row", "seq", None),
        P("row", None),
        P("seq"),
        P("seq", None),
        P("seq", None),
        P(),
        P(None, "seq"),
        P("seq", None),
        P("seq"),
        P("seq", None),
        P("seq", None),
        P("seq", None),
        P("row", "seq", None),
    )
    return jax.shard_map(
        on_device,
        mesh=mesh,
        in_specs=placed,
        out_specs=(
            P("row", "seq", None),
            P("row", "seq", None),
            P("seq"),
            P("seq", None),
            P("seq", None),
            P(),
            P(None, "seq"),
            P("seq", None),
            P("seq"),
            P("seq", None),
            P("seq", None),
            P("seq", None),
        ),
        check_vma=False,
    )
```
